32 devices in a mesh: rep: 2 (over x), tp: 16 (over z, y, core).
Axes of the slice: x: 2, y: 2, z: 4, core: 2. Of those that a mesh axis runs over, the one named last changes fastest.
Arguments:
- layer_input: bfloat16 [256, 8192], P(('rep', 'tp')), parts along dimension 0, may hold values from -400 to 400
- input_norm_gain: float32 [8192], replicated, may hold values from 0.5 to 2
- query_weight: bfloat16 [8192, 8192], P(None, 'tp'), may hold values from -1 to 1
- key_value_weight: bfloat16 [8192, 2048], P(None, 'tp'), may hold values from -1 to 1
- output_weight: bfloat16 [8192, 8192], P('tp'), may hold values from -0.125 to 0.125
- cached_key_value: bfloat16 [2, 4, 65536, 128], P(None, 'rep', 'tp'), parts along dimension 1, may hold values from -300 to 300
- adapter_down_weight: bfloat16 [32, 48, 8192], P('tp'), may hold values from -0.0625 to 0.0625
- adapter_up_weight: bfloat16 [32, 16, 10240], P('tp'), may hold values from -1.5 to 1.5
- request_adapter: int32 [4], P('rep'), parts along dimension 0, may hold values from 0 to 31
- adapter_storage_index: int32 [32], replicated, may hold values from 0 to 31, each once
- cached_length: int32 [4], P('rep'), parts along dimension 0, may hold values from 2048 to 8192, as said below
- parent_node: int32 [4, 64], P('rep'), parts along dimension 0, may hold values from 0 to 62, as said below
Outputs:
- attn_out: bfloat16 [256, 8192], P(('rep', 'tp')), parts along dimension 0
The draws below stay inside these ranges and needn't reach their ends.
There are 2 independent parts, one for each index of `rep`. The reference program is written for one: setup_inputs(seed, part) draws one part's arguments, and reference() takes and returns one part's arrays. A program takes and returns all parts, laid end to end along the dimension named above; an argument that names none is the same for every part. Nothing has to cross between parts.
Inputs may be any that keep to these rules, and one draw needn't show every extreme that they name: `cached_length`: at least one request has exactly 8192 cached tokens. parent_node[r, 0] = 0 marks the root; every other node i has a parent from i - 8 to i - 1, and the last node's parent is the node just before it.
All inputs are finite; a program needn't handle non-finite values.
Results may differ from the reference program's by a relative error of at most 0.015.
The reference program's roundings to bfloat16 on the way count: a program that leaves them out, or rounds other values in their place, can miss the bound.
Values may be sent and summed in bfloat16 or wider, within the bound.
A program may use at most 128 MiB of HBM per device.

```python
import math
import jax
import jax.numpy as jnp
from jax import lax

MODEL_WIDTH = 8192
HEADS = 64
KEY_HEADS = 8
HEAD_SIZE = 128
ADAPTER_RANK = 16
REQ = 2
TREE = 64
PREFIX = 8192
ADAPTER_COUNT = 32


def shared_columns(key):
    common_key = jax.random.fold_in(key, 5)
    shared = jax.random.normal(common_key, (MODEL_WIDTH, KEY_HEADS, 1, HEAD_SIZE))
    return jnp.clip(shared, -4.0, 4.0)


def draw_query_weight(key, part):
    shared = shared_columns(key)
    key = jax.random.fold_in(key, 51)
    shape_full = (MODEL_WIDTH, KEY_HEADS, HEADS // KEY_HEADS, HEAD_SIZE)
    own = jnp.clip(jax.random.normal(key, shape_full), -4.0, 4.0)
    values = (0.8 * shared + 0.6 * own) / math.sqrt(MODEL_WIDTH)
    return values.reshape(MODEL_WIDTH, HEADS * HEAD_SIZE).astype(jnp.bfloat16)


def draw_key_value_weight(key, part):
    shared = shared_columns(key).reshape(MODEL_WIDTH, KEY_HEADS * HEAD_SIZE)
    key = jax.random.fold_in(key, 53)
    subkeys = jax.random.split(key, 2)
    shape_half = (MODEL_WIDTH, KEY_HEADS * HEAD_SIZE)
    own = jnp.clip(jax.random.normal(subkeys[0], shape_half), -4.0, 4.0)
    value_part = jnp.clip(jax.random.normal(subkeys[1], shape_half), -4.0, 4.0)
    key_part = 0.8 * shared + 0.6 * own
    values = jnp.concatenate([key_part, value_part], axis=1) / math.sqrt(MODEL_WIDTH)
    return values.astype(jnp.bfloat16)


def draw_layer_input(key, part):
    key = jax.random.fold_in(key, 11)
    subkeys = jax.random.split(key, 3)
    row_scale = jnp.exp(jax.random.uniform(subkeys[0], (REQ * TREE, 1), minval=0.0, maxval=math.log(10.0)))
    col_scale = jnp.exp(jax.random.uniform(subkeys[1], (1, MODEL_WIDTH), minval=math.log(0.5), maxval=math.log(2.0)))
    values = jax.random.normal(subkeys[2], (REQ * TREE, MODEL_WIDTH)) * row_scale * col_scale
    return values.astype(jnp.bfloat16)


def draw_cached_key_value(key, part):
    key = jax.random.fold_in(key, 23)
    subkeys = jax.random.split(key, 2)
    shape_one = (REQ, KEY_HEADS, PREFIX, HEAD_SIZE)
    keys_drawn = jax.random.normal(subkeys[0], shape_one) * 1.5
    values_drawn = jax.random.normal(subkeys[1], shape_one)
    stacked = jnp.stack([keys_drawn, values_drawn]).reshape(2, REQ, KEY_HEADS * PREFIX, HEAD_SIZE)
    return stacked.astype(jnp.bfloat16)


def draw_cached_length(key, part):
    key = jax.random.fold_in(key, 37)
    subkeys = jax.random.split(key, 2)
    lengths = jax.random.randint(subkeys[0], (REQ,), PREFIX // 4, PREFIX + 1)
    longest = jax.random.randint(subkeys[1], (), 0, REQ)
    return jnp.where(jnp.arange(REQ) == longest, PREFIX, lengths).astype(jnp.int32)


def draw_parent_node(key, part):
    key = jax.random.fold_in(key, 41)
    offsets = jax.random.randint(key, (REQ, TREE), 1, 9)
    node_index = jnp.arange(TREE, dtype=jnp.int32)[None, :]
    parents = jnp.maximum(node_index - offsets, 0)
    parents = jnp.where(node_index == TREE - 1, TREE - 2, parents)
    return parents.astype(jnp.int32)


def block_scale(own_key, dims, shards, least, high):
    gain, own = 1.0, jax.random.fold_in(own_key, 6)
    for dim, blocks in shards:
        draws = jnp.exp(jax.random.uniform(jax.random.fold_in(own, dim), (blocks,), jnp.float32, least / len(shards), high / len(shards)))
        gain = gain * jnp.repeat(draws, dims[dim] // blocks).reshape([-1 if axis == dim else 1 for axis in range(len(dims))])
    return gain


def normal_values(own_key, dims, scale, reach, pieces=(), kind=jnp.bfloat16):
    values = jax.random.normal(own_key, dims, jnp.float32) * scale
    if len(pieces) > 0:
        values = block_scale(own_key, dims, pieces, -0.22, 0.18) * values
    return jnp.clip(values, min=-reach, max=reach).astype(kind)


def setup_inputs(seed: int = 0, part: int = 0) -> dict:
    arg_keys = jax.random.split(jax.random.key(seed), 13)
    part_keys = jax.random.split(jax.random.fold_in(arg_keys[12], part), 13)
    return {
        "layer_input": draw_layer_input(jax.random.fold_in(jax.random.fold_in(arg_keys[12], part), 71), part),
        "input_norm_gain": jnp.clip(jnp.exp(jax.random.uniform(arg_keys[1], (MODEL_WIDTH,), jnp.float32, math.log(0.5), math.log(2.0))), 0.5, 2.0),
        "query_weight": draw_query_weight(jax.random.fold_in(arg_keys[12], 71), part),
        "key_value_weight": draw_key_value_weight(jax.random.fold_in(arg_keys[12], 71), part),
        "output_weight": normal_values(arg_keys[4], (HEADS * HEAD_SIZE, MODEL_WIDTH), (HEADS * HEAD_SIZE // 4) ** -0.5, 0.125, ((0, 16),)),
        "cached_key_value": draw_cached_key_value(jax.random.fold_in(jax.random.fold_in(arg_keys[12], part), 71), part),
        "adapter_down_weight": normal_values(arg_keys[6], (ADAPTER_COUNT, 3 * ADAPTER_RANK, MODEL_WIDTH), MODEL_WIDTH ** -0.5, 0.0625, ((0, 16),)),
        "adapter_up_weight": normal_values(arg_keys[7], (ADAPTER_COUNT, ADAPTER_RANK, MODEL_WIDTH + 2 * KEY_HEADS * HEAD_SIZE), ADAPTER_RANK ** -0.5, 1.5, ((0, 16),)),
        "request_adapter": jax.random.randint(part_keys[8], (REQ,), 0, ADAPTER_COUNT).astype(jnp.int32),
        "adapter_storage_index": jax.random.permutation(arg_keys[9], ADAPTER_COUNT).astype(jnp.int32),
        "cached_length": draw_cached_length(jax.random.fold_in(jax.random.fold_in(arg_keys[12], part), 71), part),
        "parent_node": draw_parent_node(jax.random.fold_in(jax.random.fold_in(arg_keys[12], part), 71), part),
    }


epsilon = 1e-05
adapter_scale = 0.5
rope_base = 500000.0
masked_score = -1e+30

def normalize(hidden_rows, input_norm_gain):
    widened = hidden_rows.astype(jnp.float32)
    squares_mean = lax.optimization_barrier(jnp.mean(widened * widened, axis=-1, keepdims=True))
    return (widened * lax.rsqrt(squares_mean + epsilon) * input_norm_gain).astype(jnp.bfloat16)

def ancestors(parents):
    node_count = parents.shape[0]
    node_index = jnp.arange(node_count, dtype=jnp.int32)
    parent_hot = (parents[:, None] == node_index[None, :]).astype(jnp.float32)
    reached = jnp.maximum(parent_hot, jnp.eye(node_count, dtype=jnp.float32))
    for repeat in range(node_count.bit_length()):
        reached = jnp.minimum(jnp.dot(reached, reached, precision=lax.Precision.HIGHEST), 1.0)
    return reached

def rotate(vectors, positions):
    half_dim = vectors.shape[-1] // 2
    exponents = jnp.arange(half_dim, dtype=jnp.float32) * (2.0 / vectors.shape[-1])
    inverse = jnp.exp(exponents * -math.log(rope_base))
    angles = positions.astype(jnp.float32)[:, None, None] * inverse[None, None, :]
    cosine = jnp.cos(angles)
    sine_part = jnp.sin(angles)
    leading = vectors[..., :half_dim]
    second = vectors[..., half_dim:]
    return jnp.concatenate([leading * cosine - second * sine_part, second * cosine + leading * sine_part], axis=-1)

def reference(layer_input, input_norm_gain, query_weight, key_value_weight, output_weight, cached_key_value, adapter_down_weight, adapter_up_weight, request_adapter, adapter_storage_index, cached_length, parent_node):
    normed = normalize(layer_input, input_norm_gain)
    group_heads = HEADS // KEY_HEADS
    kv_width = KEY_HEADS * HEAD_SIZE
    score_scale = HEAD_SIZE ** (-0.5)
    outputs = []
    for request in range(REQ):
        storage_slot_index = adapter_storage_index[request_adapter[request]]
        down_result = adapter_down_weight[storage_slot_index]
        up_result = adapter_up_weight[storage_slot_index]
        tree_token_rows = normed[request * TREE:(request + 1) * TREE]
        low_rank = lax.dot_general(tree_token_rows, down_result, (((1,), (1,)), ((), ())), preferred_element_type=jnp.float32).astype(jnp.bfloat16)
        query_update = jnp.dot(low_rank[:, :ADAPTER_RANK], up_result[:, :MODEL_WIDTH], preferred_element_type=jnp.float32)
        query_before = (jnp.dot(tree_token_rows, query_weight, preferred_element_type=jnp.float32) + adapter_scale * query_update).astype(jnp.bfloat16)
        key_update = jnp.dot(low_rank[:, ADAPTER_RANK:2 * ADAPTER_RANK], up_result[:, MODEL_WIDTH:MODEL_WIDTH + kv_width], preferred_element_type=jnp.float32)
        value_update = jnp.dot(low_rank[:, 2 * ADAPTER_RANK:], up_result[:, MODEL_WIDTH + kv_width:], preferred_element_type=jnp.float32)
        key_value_before = (jnp.dot(tree_token_rows, key_value_weight, preferred_element_type=jnp.float32) + adapter_scale * jnp.concatenate([key_update, value_update], axis=1)).astype(jnp.bfloat16)
        reached = ancestors(parent_node[request])
        node_depth = lax.optimization_barrier(jnp.sum(reached, axis=1)).astype(jnp.int32) - 1
        positions = cached_length[request] + node_depth
        queries = rotate(query_before.astype(jnp.float32).reshape(TREE, HEADS, HEAD_SIZE), positions).astype(jnp.bfloat16)
        new_keys = rotate(key_value_before[:, :kv_width].astype(jnp.float32).reshape(TREE, KEY_HEADS, HEAD_SIZE), positions).astype(jnp.bfloat16)
        new_values = key_value_before[:, kv_width:].reshape(TREE, KEY_HEADS, HEAD_SIZE)
        cache_valid = jnp.arange(PREFIX) < cached_length[request]
        usable = jnp.concatenate([jnp.broadcast_to(cache_valid[None, :], (TREE, PREFIX)), reached > 0.5], axis=1)
        mask_rows = jnp.repeat(usable, group_heads, axis=0)
        heads_out = []
        for kv_group in range(KEY_HEADS):
            all_keys = jnp.concatenate([cached_key_value[0, request, kv_group * PREFIX:(kv_group + 1) * PREFIX], new_keys[:, kv_group]], axis=0)
            all_values = jnp.concatenate([cached_key_value[1, request, kv_group * PREFIX:(kv_group + 1) * PREFIX], new_values[:, kv_group]], axis=0)
            group_queries = queries[:, kv_group * group_heads:(kv_group + 1) * group_heads].reshape(TREE * group_heads, HEAD_SIZE)
            scores = lax.dot_general(group_queries, all_keys, (((1,), (1,)), ((), ())), preferred_element_type=jnp.float32) * score_scale
            scores = jnp.where(mask_rows, scores, masked_score)
            row_top = lax.optimization_barrier(jnp.max(scores, axis=1, keepdims=True))
            weights = jnp.where(mask_rows, jnp.exp(scores - row_top), 0.0)
            row_total = lax.optimization_barrier(jnp.sum(weights, axis=1, keepdims=True))
            blended = jnp.dot(weights.astype(jnp.bfloat16), all_values, preferred_element_type=jnp.float32) / row_total
            heads_out.append(blended.reshape(TREE, group_heads * HEAD_SIZE))
        attention = jnp.concatenate(heads_out, axis=1).astype(jnp.bfloat16)
        outputs.append(jnp.dot(attention, output_weight, preferred_element_type=jnp.float32).astype(jnp.bfloat16))
    return jnp.concatenate(outputs, axis=0)
```

```python
import math

import jax
import jax.numpy as jnp
from jax import lax
from jax.experimental import pallas as pl
from jax.experimental.pallas import tpu as pltpu
from jax.sharding import PartitionSpec as P

KEY_HEADS = 8


epsilon = 1e-05
adapter_scale = 0.5
rope_base = 500000.0
masked_score = -1e30


def broadcast(block, axis, source):
    block = jnp.where(lax.axis_index(axis) == source, block, jnp.zeros_like(block))
    return lax.psum(block, axis)


def partner_2(value, axis, stride):
    mask = 2**stride
    pairs = [(source, source ^ mask) for source in range(lax.axis_size(axis))]
    return lax.ppermute(value, axis, pairs)


def for_sending(x):

    def short(part):
        return part.astype(jnp.bfloat16) if part.dtype == jnp.float32 else part

    return jax.tree.map(short, x)


def normalize(hidden_rows, input_norm_gain):
    widened = hidden_rows.astype(jnp.float32)
    squares_mean = jnp.mean(widened * widened, axis=-1, keepdims=True)
    return (widened * lax.rsqrt(squares_mean + epsilon) * input_norm_gain).astype(jnp.bfloat16)


def ancestors(parents):
    node_count = parents.shape[0]
    node_index = jnp.arange(node_count, dtype=jnp.int32)
    parent_hot = (parents[:, None] == node_index[None, :]).astype(jnp.float32)
    reached = jnp.maximum(parent_hot, jnp.eye(node_count, dtype=jnp.float32))
    for repeat in range(node_count.bit_length()):
        reached = jnp.minimum(jnp.dot(reached, reached, precision=lax.Precision.HIGHEST), 1.0)
    return reached


def rotate(vectors, positions):
    half_dim = vectors.shape[-1] // 2
    exponents = jnp.arange(half_dim, dtype=jnp.float32) * (2.0 / vectors.shape[-1])
    inverse = jnp.exp(exponents * -math.log(rope_base))
    angles = positions.astype(jnp.float32)[:, None, None] * inverse[None, None, :]
    cosine = jnp.cos(angles)
    sine_part = jnp.sin(angles)
    leading = vectors[..., :half_dim]
    second = vectors[..., half_dim:]
    return jnp.concatenate(
        [leading * cosine - second * sine_part, second * cosine + leading * sine_part], axis=-1
    )


def project_down(tree_token_rows, down_result):
    return lax.dot_general(
        tree_token_rows, down_result, (((1,), (1,)), ((), ())), preferred_element_type=jnp.float32
    ).astype(jnp.bfloat16)


def spread(per_head, offset, width, head_dim):
    expanded = jnp.repeat(per_head, head_dim, axis=1)
    return lax.dynamic_slice_in_dim(expanded, offset, width, 1)


def combine(own_state, other_state, offset, head_dim):
    width = own_state[0].shape[1]
    new_top = jnp.maximum(own_state[1], other_state[1])
    own_factor = jnp.exp(own_state[1] - new_top)
    other_factor = jnp.exp(other_state[1] - new_top)
    new_total = own_state[2] * own_factor + other_state[2] * other_factor
    new_values = own_state[0] * spread(own_factor, offset, width, head_dim) + other_state[
        0
    ] * spread(other_factor, offset, width, head_dim)
    return (new_values, new_top, new_total)


def partial_attention(queries, all_keys, all_values, usable, group_heads):
    scores = lax.dot_general(
        queries, all_keys, (((1,), (1,)), ((), ())), preferred_element_type=jnp.float32
    ) * all_keys.shape[1] ** (-0.5)
    mask_rows = jnp.repeat(usable, group_heads, axis=0)
    scores = jnp.where(mask_rows, scores, masked_score)
    row_top = jnp.max(scores, axis=1, keepdims=True)
    weights = jnp.where(mask_rows, jnp.exp(scores - row_top), 0.0)
    row_total = jnp.sum(weights, axis=1, keepdims=True)
    blended = jnp.dot(weights.astype(jnp.bfloat16), all_values, preferred_element_type=jnp.float32)
    return (blended, row_top, row_total)


def body(
    layer_input,
    input_norm_gain,
    query_weight,
    key_value_weight,
    output_weight,
    cached_key_value,
    adapter_down_weight,
    adapter_up_weight,
    request_adapter,
    adapter_storage_index,
    cached_length,
    parent_node,
):
    devices = lax.axis_size("tp")
    device = lax.axis_index("tp")
    model_dim = query_weight.shape[0]
    query_cols = query_weight.shape[1]
    pair_cols = key_value_weight.shape[1]
    storage_slot_list = adapter_down_weight.shape[0]
    total_rank = adapter_down_weight.shape[1]
    rank_size = total_rank // 3
    requests = request_adapter.shape[0]
    tree_size = parent_node.shape[1]
    head_dim = cached_key_value.shape[3]
    block_keys = cached_key_value.shape[2]
    kv_width = pair_cols * devices // 2
    group_size = devices // KEY_HEADS
    depth_levels = group_size.bit_length() - 1
    head_group = device // group_size
    member = device % group_size
    group_width = query_cols * group_size
    group_heads = group_width // head_dim
    tree_block = tree_size // group_size
    everyone = lax.all_gather(layer_input, "tp", axis=0, tiled=True)
    normed = normalize(everyone, input_norm_gain)
    kv_start = device * pair_cols
    is_value = kv_start >= kv_width
    query_blocks = []
    pair_blocks = []
    for request in range(requests):
        storage_slot_index = adapter_storage_index[request_adapter[request]]
        owner_index = storage_slot_index // storage_slot_list
        slot_local = storage_slot_index % storage_slot_list
        request_down = lax.dynamic_index_in_dim(adapter_down_weight, slot_local, 0, keepdims=False)
        request_up = lax.dynamic_index_in_dim(adapter_up_weight, slot_local, 0, keepdims=False)
        tree_token_rows = normed[request * tree_size : (request + 1) * tree_size]
        down_result, up_result = (
            broadcast(request_down, "tp", owner_index),
            broadcast(request_up, "tp", owner_index),
        )
        low_rank = project_down(tree_token_rows, down_result)
        query_update = jnp.dot(
            low_rank[:, :rank_size],
            lax.dynamic_slice_in_dim(up_result, device * query_cols, query_cols, 1),
            preferred_element_type=jnp.float32,
        )
        query_blocks.append(
            (
                jnp.dot(tree_token_rows, query_weight, preferred_element_type=jnp.float32)
                + adapter_scale * query_update
            ).astype(jnp.bfloat16)
        )
        pair_rank = jnp.where(
            is_value, low_rank[:, 2 * rank_size :], low_rank[:, rank_size : 2 * rank_size]
        )
        paired_update = jnp.dot(
            pair_rank,
            lax.dynamic_slice_in_dim(up_result, model_dim + kv_start, pair_cols, 1),
            preferred_element_type=jnp.float32,
        )
        pair_blocks.append(
            (
                jnp.dot(tree_token_rows, key_value_weight, preferred_element_type=jnp.float32)
                + adapter_scale * paired_update
            ).astype(jnp.bfloat16)
        )
    query_local = jnp.concatenate(query_blocks, axis=0)
    pair_local = jnp.concatenate(pair_blocks, axis=0)
    pair_all = lax.all_gather(pair_local, "tp", axis=1, tiled=True)
    query_group = query_local
    for section_bit in range(depth_levels):
        partner = partner_2(query_group, "tp", section_bit)
        upper_half = member // 2**section_bit % 2 == 1
        query_group = jnp.concatenate(
            [
                jnp.where(upper_half, partner, query_group),
                jnp.where(upper_half, query_group, partner),
            ],
            axis=1,
        )
    key_cols = lax.dynamic_slice_in_dim(pair_all, head_group * head_dim, head_dim, 1)
    value_cols = lax.dynamic_slice_in_dim(pair_all, kv_width + head_group * head_dim, head_dim, 1)
    block_index = member * block_keys + jnp.arange(block_keys, dtype=jnp.int32)
    value_parts = []
    top_parts = []
    total_parts = []
    for request in range(requests):
        reached = ancestors(parent_node[request])
        node_depth = jnp.sum(reached, axis=1).astype(jnp.int32) - 1
        positions = cached_length[request] + node_depth
        request_queries = query_group[request * tree_size : (request + 1) * tree_size]
        queries = (
            rotate(
                request_queries.astype(jnp.float32).reshape(tree_size, group_heads, head_dim),
                positions,
            )
            .astype(jnp.bfloat16)
            .reshape(tree_size * group_heads, head_dim)
        )
        request_keys = key_cols[request * tree_size : (request + 1) * tree_size]
        new_keys = (
            rotate(request_keys.astype(jnp.float32).reshape(tree_size, 1, head_dim), positions)
            .astype(jnp.bfloat16)
            .reshape(tree_size, head_dim)
        )
        tree_keys = lax.dynamic_slice_in_dim(new_keys, member * tree_block, tree_block, 0)
        tree_values = lax.dynamic_slice_in_dim(
            value_cols[request * tree_size : (request + 1) * tree_size],
            member * tree_block,
            tree_block,
            0,
        )
        tree_mask = lax.dynamic_slice_in_dim(reached, member * tree_block, tree_block, 1) > 0.5
        cache_mask = jnp.broadcast_to(
            (block_index < cached_length[request])[None, :], (tree_size, block_keys)
        )
        all_keys = jnp.concatenate([cached_key_value[0, request], tree_keys], axis=0)
        all_values = jnp.concatenate([cached_key_value[1, request], tree_values], axis=0)
        blended, row_top, row_total = partial_attention(
            queries,
            all_keys,
            all_values,
            jnp.concatenate([cache_mask, tree_mask], axis=1),
            group_heads,
        )
        value_parts.append(blended.reshape(tree_size, group_width))
        top_parts.append(row_top.reshape(tree_size, group_heads))
        total_parts.append(row_total.reshape(tree_size, group_heads))
    merged = (
        jnp.concatenate(value_parts, axis=0),
        jnp.concatenate(top_parts, axis=0),
        jnp.concatenate(total_parts, axis=0),
    )
    window = group_width // group_size
    zero_offset = jnp.zeros((), jnp.int32)
    for section_bit in range(depth_levels):
        other_state = partner_2(
            (for_sending(merged[0]), for_sending(merged[1]), for_sending(merged[2])),
            "tp",
            section_bit,
        )
        merged = combine(merged, other_state, zero_offset, head_dim)
    offset = member * window
    kept_values = lax.dynamic_slice_in_dim(merged[0], offset, window, 1)
    attention = (kept_values / spread(merged[2], offset, window, head_dim)).astype(jnp.bfloat16)
    summed = lax.psum_scatter(
        jnp.dot(attention, output_weight, preferred_element_type=jnp.float32),
        "tp",
        scatter_dimension=0,
        tiled=True,
    )
    return summed.astype(jnp.bfloat16)


MESH = pl.DeviceIdType.MESH
LINE, PAIR, CORES = 4, 2, 2
OUT_CHUNKS = 4
KEY_CHUNK = 1024
lowest = -1e29


def fused_kernel(
    slot_of, adapter_of, length_of, rows_in, gain, parents, inverse, down, up,
    query_weight, pair_weight, out_weight, cache, out,
    w_query, w_pair, w_out, kv_cache, rows_all, normed, down_here, up_here,
    up_send, up_sib, up_mid, up_y, up_low, up_z, low_send, low_recv,
    query_buf, pair_own, tree_keys, tree_values, blended, tops, totals,
    merge_send, merge_recv, attention, part, part_sib, y_send, y_recv, z_send, z_recv,
    load_sem, rows_send, rows_recv, up_ssem, up_rsem, low_ssem, low_rsem,
    query_sem, pair_ssem, pair_rsem, merge_ssem, merge_rsem,
    sib_ssem, sib_rsem, y_ssem, y_rsem, z_ssem, z_rsem,
):
    me = lax.axis_index("tp")
    z, y, c = me // (PAIR * CORES), me // CORES % PAIR, me % CORES
    count = LINE * PAIR * CORES

    def at(zz, yy, cc):
        return (zz * PAIR + yy) * CORES + cc

    def hop(k):
        return (z + k) % LINE

    def remote(src, dst, ssem, rsem, target):
        return pltpu.make_async_remote_copy(
            src_ref=src, dst_ref=dst, send_sem=ssem, recv_sem=rsem,
            device_id={"tp": target}, device_id_type=MESH,
        )

    sib, ypart = at(z, y, 1 - c), at(z, 1 - y, c)
    loads = [
        pltpu.make_async_copy(a, b, load_sem.at[i])
        for i, (a, b) in enumerate([
            (up, up_here), (down, down_here), (query_weight, w_query),
            (pair_weight, w_pair), (cache, kv_cache), (out_weight, w_out)])
    ]
    for load in loads:
        load.start()
    barrier = pltpu.get_barrier_semaphore()
    for k in range(1, count):
        pl.semaphore_signal(
            barrier, inc=1, device_id={"tp": (me + k) % count}, device_id_type=MESH)
    rows_all[me] = rows_in[...]
    pl.semaphore_wait(barrier, count - 1)

    sent = []

    def push_rows(block, target):
        copy = remote(rows_all.at[block], rows_all.at[block],
                      rows_send.at[len(sent)], rows_recv.at[block], target)
        copy.start()
        sent.append(copy)

    def take_rows(block):
        remote(rows_all.at[block], rows_all.at[block], rows_send.at[0],
               rows_recv.at[block], sib).wait_recv()

    for k in range(1, LINE):
        push_rows(me, at(hop(k), y, c))
    push_rows(me, ypart)
    push_rows(me, sib)

    requests, tree = 2, 64
    rank, slots = up_here.shape[1], up_here.shape[0]
    q_cols, p_cols = w_query.shape[1], w_pair.shape[1]
    width = q_cols * count
    chosen = []
    for r in range(requests):
        slot = slot_of[adapter_of[r]]
        chosen.append([slot == me * slots + s for s in range(slots)])
    loads[0].wait()
    for r in range(requests):
        picked = jnp.zeros(up_here.shape[1:], up_here.dtype)
        for s in range(slots):
            picked = jnp.where(chosen[r][s], up_here[s], picked)
        for d in range(count):
            zz, yy, cc = d // 4, d // 2 % 2, d % 2
            up_send[cc, yy, zz, r * rank:(r + 1) * rank, :q_cols] = (
                picked[:, d * q_cols:(d + 1) * q_cols])
            up_send[cc, yy, zz, r * rank:(r + 1) * rank, q_cols:] = (
                picked[:, width + d * p_cols:width + (d + 1) * p_cols])
    up_first = remote(up_send.at[1 - c], up_sib, up_ssem.at[0], up_rsem.at[0], sib)
    up_first.start()

    for k in range(1, LINE):
        block = at(hop(k), y, c)
        take_rows(block)
        push_rows(block, ypart)
        push_rows(block, sib)

    up_first.wait()
    up_mid[...] = up_send[c] + up_sib[...]
    up_second = remote(up_mid.at[1 - y], up_y, up_ssem.at[1], up_rsem.at[1], ypart)
    up_second.start()

    reached, cosines, sines = [], [], []
    node = lax.broadcasted_iota(jnp.int32, (tree, tree), 1)
    own = lax.broadcasted_iota(jnp.int32, (tree, tree), 0)
    for r in range(requests):
        hot = jnp.where((parents[r] == node) | (own == node), 1.0, 0.0)
        for _ in range(tree.bit_length()):
            short = hot.astype(jnp.bfloat16)
            hot = jnp.minimum(
                jnp.dot(short, short, preferred_element_type=jnp.float32), 1.0)
        reached.append(hot)
        depth = jnp.sum(hot, axis=1, keepdims=True).astype(jnp.int32) - 1
        position = (depth + length_of[r]).astype(jnp.float32)
        angles = position * inverse[...]
        cosines.append(jnp.cos(angles))
        sines.append(jnp.sin(angles))

    for k in range(LINE):
        block = at(hop(k), 1 - y, c)
        take_rows(block)
        push_rows(block, sib)

    up_second.wait()
    up_low[...] = up_mid[y] + up_y[...]
    up_third = []
    for k in range(1, LINE):
        copy = remote(up_low.at[hop(k)], up_z.at[k - 1], up_ssem.at[1 + k], up_rsem.at[1 + k],
                      at(hop(k), y, c))
        copy.start()
        up_third.append(copy)

    for k in range(LINE):
        for yy in (y, 1 - y):
            take_rows(at(hop(k), yy, 1 - c))

    half = rows_all.shape[2]

    def norm_step(k, carry):
        parts = []
        for j in range(2):
            block = rows_all[2 * k + j].astype(jnp.float32)
            squares = jnp.sum(block * block, axis=1, keepdims=True)
            scale = lax.rsqrt((squares[:8] + squares[8:]) / (2 * half) + epsilon)
            parts.append((block[:8] * scale, block[8:] * scale))
        for h in range(2):
            both = jnp.concatenate([parts[0][h], parts[1][h]], axis=0)
            cols = slice(h * half, (h + 1) * half)
            normed[pl.ds(pl.multiple_of(k * 16, 16), 16), cols] = (
                both * gain[:, cols]).astype(jnp.bfloat16)
        return carry

    lax.fori_loop(0, count // 2, norm_step, 0)

    nt = (((1,), (1,)), ((), ()))
    tn = (((0,), (0,)), ((), ()))
    loads[1].wait()
    token = lax.broadcasted_iota(jnp.int32, (1, requests * tree), 1)
    low = jnp.zeros((down_here.shape[1], requests * tree), jnp.float32)
    for s in range(slots):
        flag = jnp.where(token < tree, chosen[0][s].astype(jnp.int32),
                         chosen[1][s].astype(jnp.int32))
        value = lax.dot_general(down_here[s], normed[...], nt,
                                preferred_element_type=jnp.float32)
        low = jnp.where(flag == 1, value, low)
    low_send[0] = low.astype(jnp.bfloat16)
    first = remote(low_send.at[0], low_recv.at[0], low_ssem.at[0], low_rsem.at[0], sib)
    first.start()

    loads[2].wait()
    loads[3].wait()
    steps = 4
    depth = w_query.shape[0] // steps
    q_acc = jnp.zeros((requests * tree, q_cols), jnp.float32)
    p_acc = jnp.zeros((requests * tree, p_cols), jnp.float32)
    pending = first
    thirds = []
    for step in range(steps):
        cut = slice(step * depth, (step + 1) * depth)
        q_acc += jnp.dot(normed[:, cut], w_query[cut], preferred_element_type=jnp.float32)
        p_acc += jnp.dot(normed[:, cut], w_pair[cut], preferred_element_type=jnp.float32)
        if step == 0:
            first.wait()
            low_send[1] = low_send[0] + low_recv[0]
            second = remote(low_send.at[1], low_recv.at[1], low_ssem.at[1], low_rsem.at[1], ypart)
            second.start()
        if step == 1:
            second.wait()
            low_send[2] = low_send[1] + low_recv[1]
            for k in range(1, LINE):
                copy = remote(low_send.at[2], low_recv.at[1 + k], low_ssem.at[1 + k],
                              low_rsem.at[1 + k], at(hop(k), y, c))
                copy.start()
                thirds.append(copy)
    for copy in thirds + up_third:
        copy.wait()
    low_all = low_send[2] + low_recv[2] + low_recv[3] + low_recv[4]
    up_all = up_low[z] + up_z[0] + up_z[1] + up_z[2]
    is_value = me >= count // 2
    q_heads = q_cols // 128

    def rotated(vectors, r):
        front, back = vectors[:, :tree], vectors[:, tree:]
        return jnp.concatenate(
            [front * cosines[r] - back * sines[r], back * cosines[r] + front * sines[r]], axis=1)

    for r in range(requests):
        rows = slice(r * tree, (r + 1) * tree)
        low_r = low_all[:, rows]
        up_r = up_all[r * rank:(r + 1) * rank]
        update = lax.dot_general(low_r[:rank], up_r[:, :q_cols], tn,
                                 preferred_element_type=jnp.float32)
        q_pre = (q_acc[rows] + adapter_scale * update).astype(jnp.bfloat16).astype(jnp.float32)
        for h in range(q_heads):
            query_buf[c, r, h] = rotated(q_pre[:, h * 128:(h + 1) * 128], r).astype(jnp.bfloat16)
        pair_low = jnp.where(is_value, low_r[2 * rank:], low_r[rank:2 * rank])
        update = lax.dot_general(pair_low, up_r[:, q_cols:], tn,
                                 preferred_element_type=jnp.float32)
        p_pre = (p_acc[rows] + adapter_scale * update).astype(jnp.bfloat16).astype(jnp.float32)
        final = jnp.where(is_value, p_pre, rotated(p_pre, r)).astype(jnp.bfloat16)
        for m in range(CORES):
            pair_own[m, r] = final[m * (tree // 2):(m + 1) * (tree // 2)]

    q_copy = remote(query_buf.at[c], query_buf.at[c], query_sem.at[0], query_sem.at[1], sib)
    q_copy.start()
    group = me % (count // 2)
    for is_v, landing in ((0, tree_keys), (1, tree_values)):
        for m in range(CORES):
            target = group * CORES + m

            @pl.when((is_value == (is_v == 1)) & (target != me))
            def _():
                remote(pair_own.at[m], landing, pair_ssem.at[m], pair_rsem.at[is_v], target).start()

            @pl.when((is_value == (is_v == 1)) & (target == me))
            def _():
                landing[...] = pair_own[m]

    for m in range(CORES):
        @pl.when(group * CORES + m != me)
        def _():
            remote(pair_own.at[m], tree_keys, pair_ssem.at[m], pair_rsem.at[0], sib).wait_send()

    @pl.when(me // CORES != me)
    def _():
        remote(pair_own.at[0], tree_keys, pair_ssem.at[0], pair_rsem.at[0], sib).wait_recv()

    @pl.when(me // CORES + count // 2 != me)
    def _():
        remote(pair_own.at[0], tree_values, pair_ssem.at[0], pair_rsem.at[1], sib).wait_recv()

    q_copy.wait_send()
    remote(query_buf.at[1 - c], query_buf.at[1 - c], query_sem.at[0], query_sem.at[1],
           sib).wait_recv()
    for copy in sent:
        copy.wait_send()

    loads[4].wait()
    heads = CORES * q_heads
    block_rows = heads * tree
    scale = 128 ** -0.5
    slots_here = kv_cache.shape[2]
    for r in range(requests):
        queries = query_buf[:, r].reshape(block_rows, 128)
        mask = jnp.where(c == 0, reached[r][:, :tree // 2], reached[r][:, tree // 2:])
        mask = jnp.concatenate([mask] * heads, axis=0)
        scores = lax.dot_general(queries, tree_keys[r], nt,
                                 preferred_element_type=jnp.float32) * scale
        scores = jnp.where(mask > 0.5, scores, masked_score)
        top = jnp.maximum(jnp.max(scores, axis=1, keepdims=True), lowest)
        weights = jnp.exp(scores - top)
        total = jnp.sum(weights, axis=1, keepdims=True)
        blend = jnp.dot(weights.astype(jnp.bfloat16), tree_values[r],
                        preferred_element_type=jnp.float32)
        limit = length_of[r] - c * slots_here

        def key_step(j, carry):
            top, total, blend = carry
            start = pl.multiple_of(j * KEY_CHUNK, KEY_CHUNK)
            scores = lax.dot_general(queries, kv_cache[0, r, pl.ds(start, KEY_CHUNK)], nt,
                                     preferred_element_type=jnp.float32) * scale
            column = lax.broadcasted_iota(jnp.int32, (1, KEY_CHUNK), 1) + start
            scores = jnp.where(column < limit, scores, masked_score)
            new_top = jnp.maximum(top, jnp.max(scores, axis=1, keepdims=True))
            weights = jnp.exp(scores - new_top)
            factor = jnp.exp(top - new_top)
            total = total * factor + jnp.sum(weights, axis=1, keepdims=True)
            blend = blend * factor + jnp.dot(
                weights.astype(jnp.bfloat16), kv_cache[1, r, pl.ds(start, KEY_CHUNK)],
                preferred_element_type=jnp.float32)
            return new_top, total, blend

        top, total, blend = lax.fori_loop(0, slots_here // KEY_CHUNK, key_step,
                                          (top, total, blend))
        top = jnp.broadcast_to(top, blend.shape)
        total = jnp.broadcast_to(total, blend.shape)
        mine = block_rows // CORES
        for m in range(CORES):
            cut = slice(m * mine, (m + 1) * mine)
            merge_send[m, r, 0] = blend[cut]
            merge_send[m, r, 1] = top[cut]
            merge_send[m, r, 2] = total[cut]
        remote(merge_send.at[1 - c, r], merge_recv.at[r], merge_ssem.at[r], merge_rsem.at[r],
               sib).start()

    loads[5].wait()
    for r in range(requests):
        remote(merge_send.at[1 - c, r], merge_recv.at[r], merge_ssem.at[r], merge_rsem.at[r],
               sib).wait()
        top = jnp.maximum(merge_send[c, r, 1], merge_recv[r, 1])
        f_own, f_other = jnp.exp(merge_send[c, r, 1] - top), jnp.exp(merge_recv[r, 1] - top)
        total = merge_send[c, r, 2] * f_own + merge_recv[r, 2] * f_other
        value = (merge_send[c, r, 0] * f_own + merge_recv[r, 0] * f_other) / total
        value = value.astype(jnp.bfloat16)
        for h in range(q_heads):
            attention[r * tree:(r + 1) * tree, h * 128:(h + 1) * 128] = (
                value[h * tree:(h + 1) * tree])

    columns = w_out.shape[1] // OUT_CHUNKS

    def sib_copy(n):
        return remote(part.at[n, 1 - c], part_sib.at[n], sib_ssem.at[n], sib_rsem.at[n], sib)

    def y_copy(n):
        return remote(y_send.at[n], y_recv.at[n], y_ssem.at[n], y_rsem.at[n], ypart)

    def z_copy(n, k):
        return remote(z_send.at[n, hop(k)], z_recv.at[n, k - 1], z_ssem.at[n, k - 1],
                      z_rsem.at[n, k - 1], at(hop(k), y, c))

    for n in range(OUT_CHUNKS):
        product = jnp.dot(attention[...], w_out[:, n * columns:(n + 1) * columns],
                          preferred_element_type=jnp.float32)
        for d in range(count):
            part[n, d % 2, d // 2 % 2, d // 4] = product[d * 8:(d + 1) * 8]
        sib_copy(n).start()
    for n in range(OUT_CHUNKS):
        sib_copy(n).wait()
        away = part[n, c, 1 - y] + part_sib[n, 1 - y]
        y_send[n] = away.reshape(LINE * 8, columns).astype(jnp.bfloat16)
        y_copy(n).start()
    for n in range(OUT_CHUNKS):
        y_copy(n).wait()
        held = (part[n, c, y] + part_sib[n, y]) + y_recv[n].astype(jnp.float32).reshape(
            LINE, 8, columns)
        part_sib[n, 0] = held
        for d in range(LINE):
            z_send[n, d] = jnp.concatenate(
                [held[d, :, :columns // 2], held[d, :, columns // 2:]], axis=0).astype(jnp.bfloat16)
        for k in range(1, LINE):
            z_copy(n, k).start()
    for n in range(OUT_CHUNKS):
        total = part_sib[n, 0, z]
        for k in range(1, LINE):
            z_copy(n, k).wait()
            landed = z_recv[n, k - 1].astype(jnp.float32)
            total = total + jnp.concatenate([landed[:8], landed[8:]], axis=1)
        out[:, n * columns:(n + 1) * columns] = total.astype(jnp.bfloat16)


def fused_body(
    layer_input, input_norm_gain, query_weight, key_value_weight, output_weight,
    cached_key_value, adapter_down_weight, adapter_up_weight, request_adapter,
    adapter_storage_index, cached_length, parent_node,
):
    rows, model = layer_input.shape
    half = model // 2
    packed = layer_input.reshape(rows, 2, half).transpose(1, 0, 2).reshape(2 * rows, half)
    exponents = jnp.arange(64, dtype=jnp.float32) * (2.0 / 128)
    inverse = jnp.exp(exponents * -math.log(rope_base))[None]
    bf, f32 = jnp.bfloat16, jnp.float32
    count = 16
    rank = adapter_up_weight.shape[1]
    ranks = adapter_down_weight.shape[1]
    cols = query_weight.shape[1] + key_value_weight.shape[1]
    columns = model // OUT_CHUNKS
    dma = pltpu.SemaphoreType.DMA
    n = OUT_CHUNKS
    scratch = [
        pltpu.VMEM(query_weight.shape, bf), pltpu.VMEM(key_value_weight.shape, bf),
        pltpu.VMEM(output_weight.shape, bf), pltpu.VMEM(cached_key_value.shape, bf),
        pltpu.VMEM((count, 2 * rows, half), bf), pltpu.VMEM((count * rows, model), bf),
        pltpu.VMEM(adapter_down_weight.shape, bf), pltpu.VMEM(adapter_up_weight.shape, bf),
        pltpu.VMEM((2, 2, 4, 2 * rank, cols), bf), pltpu.VMEM((2, 4, 2 * rank, cols), bf),
        pltpu.VMEM((2, 4, 2 * rank, cols), bf), pltpu.VMEM((4, 2 * rank, cols), bf),
        pltpu.VMEM((4, 2 * rank, cols), bf), pltpu.VMEM((3, 2 * rank, cols), bf),
        pltpu.VMEM((3, ranks, 128), bf), pltpu.VMEM((5, ranks, 128), bf),
        pltpu.VMEM((2, 2, 4, 64, 128), bf), pltpu.VMEM((2, 2, 32, 128), bf),
        pltpu.VMEM((2, 32, 128), bf), pltpu.VMEM((2, 32, 128), bf),
        pltpu.VMEM((8, 128), f32), pltpu.VMEM((8, 128), f32), pltpu.VMEM((8, 128), f32),
        pltpu.VMEM((2, 2, 3, 256, 128), f32), pltpu.VMEM((2, 3, 256, 128), f32),
        pltpu.VMEM((128, 512), bf),
        pltpu.VMEM((n, 2, 2, 4, 8, columns), f32), pltpu.VMEM((n, 2, 4, 8, columns), f32),
        pltpu.VMEM((n, 32, columns), bf), pltpu.VMEM((n, 32, columns), bf),
        pltpu.VMEM((n, 4, 16, columns // 2), bf), pltpu.VMEM((n, 3, 16, columns // 2), bf),
        dma((6,)), dma((15,)), dma((count,)), dma((5,)), dma((5,)), dma((5,)), dma((5,)),
        dma((2,)), dma((2,)), dma((2,)), dma((2,)), dma((2,)),
        dma((n,)), dma((n,)), dma((n,)), dma((n,)), dma((n, 3)), dma((n, 3)),
    ]
    smem = pl.BlockSpec(memory_space=pltpu.SMEM)
    vmem = pl.BlockSpec(memory_space=pltpu.VMEM)
    hbm = pl.BlockSpec(memory_space=pl.ANY)
    return pl.pallas_call(
        fused_kernel,
        out_shape=jax.ShapeDtypeStruct((rows, model), bf),
        in_specs=[smem] * 3 + [vmem] * 4 + [hbm] * 6,
        out_specs=vmem,
        scratch_shapes=scratch,
        compiler_params=pltpu.CompilerParams(
            collective_id=0, has_side_effects=True, vmem_limit_bytes=60 * 2**20),
        cost_estimate=pl.CostEstimate(
            flops=5 * 10**9, bytes_accessed=25 * 2**20, transcendentals=4 * 2**20),
        name="fused_layer",
    )(adapter_storage_index, request_adapter, cached_length, packed, input_norm_gain[None],
      parent_node[:, :, None], inverse, adapter_down_weight, adapter_up_weight,
      query_weight, key_value_weight, output_weight, cached_key_value)


def solution(mesh):
    in_specs = (
        P(("rep", "tp"), None),
        P(),
        P(None, "tp"),
        P(None, "tp"),
        P("tp", None),
        P(None, "rep", "tp", None),
        P("tp", None, None),
        P("tp", None, None),
        P("rep"),
        P(),
        P("rep"),
        P("rep", None),
    )
    out_specs = P(("rep", "tp"), None)
    fused = mesh.shape["tp"] == 16 and mesh.shape["rep"] == 2
    return jax.shard_map(fused_body if fused else body, mesh=mesh, in_specs=in_specs, out_specs=out_specs, check_vma=False)
```

```python
import math

import jax
import numpy as np
import jax.numpy as jnp
from jax import lax
from jax.experimental import pallas as pl
from jax.experimental.pallas import tpu as pltpu
from jax.sharding import PartitionSpec as P

KEY_HEADS = 8


epsilon = 1e-05
adapter_scale = 0.5
rope_base = 500000.0
masked_score = -1e30


def broadcast(block, axis, source):
    block = jnp.where(lax.axis_index(axis) == source, block, jnp.zeros_like(block))
    return lax.psum(block, axis)


def partner_2(value, axis, stride):
    mask = 2**stride
    pairs = [(source, source ^ mask) for source in range(lax.axis_size(axis))]
    return lax.ppermute(value, axis, pairs)


def for_sending(x):

    def short(part):
        return part.astype(jnp.bfloat16) if part.dtype == jnp.float32 else part

    return jax.tree.map(short, x)


def normalize(hidden_rows, input_norm_gain):
    widened = hidden_rows.astype(jnp.float32)
    squares_mean = jnp.mean(widened * widened, axis=-1, keepdims=True)
    return (widened * lax.rsqrt(squares_mean + epsilon) * input_norm_gain).astype(jnp.bfloat16)


def ancestors(parents):
    node_count = parents.shape[0]
    node_index = jnp.arange(node_count, dtype=jnp.int32)
    parent_hot = (parents[:, None] == node_index[None, :]).astype(jnp.float32)
    reached = jnp.maximum(parent_hot, jnp.eye(node_count, dtype=jnp.float32))
    for repeat in range(node_count.bit_length()):
        reached = jnp.minimum(jnp.dot(reached, reached, precision=lax.Precision.HIGHEST), 1.0)
    return reached


def rotate(vectors, positions):
    half_dim = vectors.shape[-1] // 2
    exponents = jnp.arange(half_dim, dtype=jnp.float32) * (2.0 / vectors.shape[-1])
    inverse = jnp.exp(exponents * -math.log(rope_base))
    angles = positions.astype(jnp.float32)[:, None, None] * inverse[None, None, :]
    cosine = jnp.cos(angles)
    sine_part = jnp.sin(angles)
    leading = vectors[..., :half_dim]
    second = vectors[..., half_dim:]
    return jnp.concatenate(
        [leading * cosine - second * sine_part, second * cosine + leading * sine_part], axis=-1
    )


def project_down(tree_token_rows, down_result):
    return lax.dot_general(
        tree_token_rows, down_result, (((1,), (1,)), ((), ())), preferred_element_type=jnp.float32
    ).astype(jnp.bfloat16)


def spread(per_head, offset, width, head_dim):
    expanded = jnp.repeat(per_head, head_dim, axis=1)
    return lax.dynamic_slice_in_dim(expanded, offset, width, 1)


def combine(own_state, other_state, offset, head_dim):
    width = own_state[0].shape[1]
    new_top = jnp.maximum(own_state[1], other_state[1])
    own_factor = jnp.exp(own_state[1] - new_top)
    other_factor = jnp.exp(other_state[1] - new_top)
    new_total = own_state[2] * own_factor + other_state[2] * other_factor
    new_values = own_state[0] * spread(own_factor, offset, width, head_dim) + other_state[
        0
    ] * spread(other_factor, offset, width, head_dim)
    return (new_values, new_top, new_total)


def partial_attention(queries, all_keys, all_values, usable, group_heads):
    scores = lax.dot_general(
        queries, all_keys, (((1,), (1,)), ((), ())), preferred_element_type=jnp.float32
    ) * all_keys.shape[1] ** (-0.5)
    mask_rows = jnp.repeat(usable, group_heads, axis=0)
    scores = jnp.where(mask_rows, scores, masked_score)
    row_top = jnp.max(scores, axis=1, keepdims=True)
    weights = jnp.where(mask_rows, jnp.exp(scores - row_top), 0.0)
    row_total = jnp.sum(weights, axis=1, keepdims=True)
    blended = jnp.dot(weights.astype(jnp.bfloat16), all_values, preferred_element_type=jnp.float32)
    return (blended, row_top, row_total)


def body(
    layer_input,
    input_norm_gain,
    query_weight,
    key_value_weight,
    output_weight,
    cached_key_value,
    adapter_down_weight,
    adapter_up_weight,
    request_adapter,
    adapter_storage_index,
    cached_length,
    parent_node,
):
    devices = lax.axis_size("tp")
    device = lax.axis_index("tp")
    model_dim = query_weight.shape[0]
    query_cols = query_weight.shape[1]
    pair_cols = key_value_weight.shape[1]
    storage_slot_list = adapter_down_weight.shape[0]
    total_rank = adapter_down_weight.shape[1]
    rank_size = total_rank // 3
    requests = request_adapter.shape[0]
    tree_size = parent_node.shape[1]
    head_dim = cached_key_value.shape[3]
    block_keys = cached_key_value.shape[2]
    kv_width = pair_cols * devices // 2
    group_size = devices // KEY_HEADS
    depth_levels = group_size.bit_length() - 1
    head_group = device // group_size
    member = device % group_size
    group_width = query_cols * group_size
    group_heads = group_width // head_dim
    tree_block = tree_size // group_size
    everyone = lax.all_gather(layer_input, "tp", axis=0, tiled=True)
    normed = normalize(everyone, input_norm_gain)
    kv_start = device * pair_cols
    is_value = kv_start >= kv_width
    query_blocks = []
    pair_blocks = []
    for request in range(requests):
        storage_slot_index = adapter_storage_index[request_adapter[request]]
        owner_index = storage_slot_index // storage_slot_list
        slot_local = storage_slot_index % storage_slot_list
        request_down = lax.dynamic_index_in_dim(adapter_down_weight, slot_local, 0, keepdims=False)
        request_up = lax.dynamic_index_in_dim(adapter_up_weight, slot_local, 0, keepdims=False)
        tree_token_rows = normed[request * tree_size : (request + 1) * tree_size]
        down_result, up_result = (
            broadcast(request_down, "tp", owner_index),
            broadcast(request_up, "tp", owner_index),
        )
        low_rank = project_down(tree_token_rows, down_result)
        query_update = jnp.dot(
            low_rank[:, :rank_size],
            lax.dynamic_slice_in_dim(up_result, device * query_cols, query_cols, 1),
            preferred_element_type=jnp.float32,
        )
        query_blocks.append(
            (
                jnp.dot(tree_token_rows, query_weight, preferred_element_type=jnp.float32)
                + adapter_scale * query_update
            ).astype(jnp.bfloat16)
        )
        pair_rank = jnp.where(
            is_value, low_rank[:, 2 * rank_size :], low_rank[:, rank_size : 2 * rank_size]
        )
        paired_update = jnp.dot(
            pair_rank,
            lax.dynamic_slice_in_dim(up_result, model_dim + kv_start, pair_cols, 1),
            preferred_element_type=jnp.float32,
        )
        pair_blocks.append(
            (
                jnp.dot(tree_token_rows, key_value_weight, preferred_element_type=jnp.float32)
                + adapter_scale * paired_update
            ).astype(jnp.bfloat16)
        )
    query_local = jnp.concatenate(query_blocks, axis=0)
    pair_local = jnp.concatenate(pair_blocks, axis=0)
    pair_all = lax.all_gather(pair_local, "tp", axis=1, tiled=True)
    query_group = query_local
    for section_bit in range(depth_levels):
        partner = partner_2(query_group, "tp", section_bit)
        upper_half = member // 2**section_bit % 2 == 1
        query_group = jnp.concatenate(
            [
                jnp.where(upper_half, partner, query_group),
                jnp.where(upper_half, query_group, partner),
            ],
            axis=1,
        )
    key_cols = lax.dynamic_slice_in_dim(pair_all, head_group * head_dim, head_dim, 1)
    value_cols = lax.dynamic_slice_in_dim(pair_all, kv_width + head_group * head_dim, head_dim, 1)
    block_index = member * block_keys + jnp.arange(block_keys, dtype=jnp.int32)
    value_parts = []
    top_parts = []
    total_parts = []
    for request in range(requests):
        reached = ancestors(parent_node[request])
        node_depth = jnp.sum(reached, axis=1).astype(jnp.int32) - 1
        positions = cached_length[request] + node_depth
        request_queries = query_group[request * tree_size : (request + 1) * tree_size]
        queries = (
            rotate(
                request_queries.astype(jnp.float32).reshape(tree_size, group_heads, head_dim),
                positions,
            )
            .astype(jnp.bfloat16)
            .reshape(tree_size * group_heads, head_dim)
        )
        request_keys = key_cols[request * tree_size : (request + 1) * tree_size]
        new_keys = (
            rotate(request_keys.astype(jnp.float32).reshape(tree_size, 1, head_dim), positions)
            .astype(jnp.bfloat16)
            .reshape(tree_size, head_dim)
        )
        tree_keys = lax.dynamic_slice_in_dim(new_keys, member * tree_block, tree_block, 0)
        tree_values = lax.dynamic_slice_in_dim(
            value_cols[request * tree_size : (request + 1) * tree_size],
            member * tree_block,
            tree_block,
            0,
        )
        tree_mask = lax.dynamic_slice_in_dim(reached, member * tree_block, tree_block, 1) > 0.5
        cache_mask = jnp.broadcast_to(
            (block_index < cached_length[request])[None, :], (tree_size, block_keys)
        )
        all_keys = jnp.concatenate([cached_key_value[0, request], tree_keys], axis=0)
        all_values = jnp.concatenate([cached_key_value[1, request], tree_values], axis=0)
        blended, row_top, row_total = partial_attention(
            queries,
            all_keys,
            all_values,
            jnp.concatenate([cache_mask, tree_mask], axis=1),
            group_heads,
        )
        value_parts.append(blended.reshape(tree_size, group_width))
        top_parts.append(row_top.reshape(tree_size, group_heads))
        total_parts.append(row_total.reshape(tree_size, group_heads))
    merged = (
        jnp.concatenate(value_parts, axis=0),
        jnp.concatenate(top_parts, axis=0),
        jnp.concatenate(total_parts, axis=0),
    )
    window = group_width // group_size
    zero_offset = jnp.zeros((), jnp.int32)
    for section_bit in range(depth_levels):
        other_state = partner_2(
            (for_sending(merged[0]), for_sending(merged[1]), for_sending(merged[2])),
            "tp",
            section_bit,
        )
        merged = combine(merged, other_state, zero_offset, head_dim)
    offset = member * window
    kept_values = lax.dynamic_slice_in_dim(merged[0], offset, window, 1)
    attention = (kept_values / spread(merged[2], offset, window, head_dim)).astype(jnp.bfloat16)
    summed = lax.psum_scatter(
        jnp.dot(attention, output_weight, preferred_element_type=jnp.float32),
        "tp",
        scatter_dimension=0,
        tiled=True,
    )
    return summed.astype(jnp.bfloat16)


MESH = pl.DeviceIdType.MESH
LINE, PAIR, CORES = 4, 2, 2
OUT_CHUNKS = 4
KEY_CHUNK = 1024
lowest = -1e29


def fused_kernel(
    slot_of, adapter_of, length_of, rows_in, gain, parents, inverse, down, up,
    query_weight, pair_weight, out_weight, cache, out,
    w_query, w_pair, w_out, kv_cache, rows_all, normed, down_here, up_here,
    up_send, up_sib, up_mid, up_y, up_low, up_z, low_send, low_recv,
    query_buf, pair_own, tree_keys, tree_values,
    merge_send, merge_recv, attention, part, part_sib, y_send, y_recv, z_send, z_recv,
    load_sem, rows_send, line_send, rows_recv, up_ssem, up_rsem, low_ssem, low_rsem,
    query_sem, pair_ssem, pair_rsem, merge_ssem, merge_rsem,
    sib_ssem, sib_rsem, y_ssem, y_rsem, z_ssem, z_rsem,
):
    me = lax.axis_index("tp")
    z, y, c = me // (PAIR * CORES), me // CORES % PAIR, me % CORES
    count = LINE * PAIR * CORES

    def at(zz, yy, cc):
        return (zz * PAIR + yy) * CORES + cc

    def hop(k):
        return (z + k) % LINE

    def remote(src, dst, ssem, rsem, target):
        return pltpu.make_async_remote_copy(
            src_ref=src, dst_ref=dst, send_sem=ssem, recv_sem=rsem,
            device_id={"tp": target}, device_id_type=MESH,
        )

    sib, ypart = at(z, y, 1 - c), at(z, 1 - y, c)
    loads = [
        pltpu.make_async_copy(a, b, load_sem.at[i])
        for i, (a, b) in enumerate([
            (up, up_here), (down, down_here), (query_weight, w_query),
            (pair_weight, w_pair), (cache, kv_cache), (out_weight, w_out)])
    ]
    for load in loads:
        load.start()
    barrier = pltpu.get_barrier_semaphore()
    for k in range(1, count):
        pl.semaphore_signal(
            barrier, inc=1, device_id={"tp": (me + k) % count}, device_id_type=MESH)
    rows_all[me] = rows_in[...]
    pl.semaphore_wait(barrier, count - 1)

    sent = []

    def push_rows(block, target):
        copy = remote(rows_all.at[block], rows_all.at[block],
                      rows_send.at[len(sent)], rows_recv.at[block], target)
        copy.start()
        sent.append(copy)

    def take_rows(block):
        remote(rows_all.at[block], rows_all.at[block], rows_send.at[0],
               rows_recv.at[block], sib).wait_recv()

    def line_copy(distance, side):
        block = at(z - side * distance, y, c)
        return remote(rows_all.at[block], rows_all.at[block],
                      line_send.at[distance, (side + 1) // 2, 0], rows_recv.at[block],
                      at(z + side, y, c))

    def fan_copy(distance, side, target, place):
        block = at(z - side * distance, y, c)
        return remote(rows_all.at[block], rows_all.at[block],
                      line_send.at[distance, (side + 1) // 2, place], rows_recv.at[block], target)

    def on_line(place):
        return (place >= 0) & (place < LINE)

    for side in (1, -1):
        @pl.when(on_line(z + side))
        def _():
            line_copy(0, side).start()
    push_rows(me, ypart)
    push_rows(me, sib)

    requests, tree = 2, 64
    rank, slots = up_here.shape[1], up_here.shape[0]
    q_cols, p_cols = w_query.shape[1], w_pair.shape[1]
    width = q_cols * count
    chosen = []
    for r in range(requests):
        slot = slot_of[adapter_of[r]]
        chosen.append([slot == me * slots + s for s in range(slots)])
    loads[0].wait()
    for r in range(requests):
        picked = jnp.zeros(up_here.shape[1:], up_here.dtype)
        for s in range(slots):
            picked = jnp.where(chosen[r][s], up_here[s], picked)
        for d in range(count):
            zz, yy, cc = d // 4, d // 2 % 2, d % 2
            up_send[cc, yy, zz, r * rank:(r + 1) * rank, :q_cols] = (
                picked[:, d * q_cols:(d + 1) * q_cols])
            up_send[cc, yy, zz, r * rank:(r + 1) * rank, q_cols:] = (
                picked[:, width + d * p_cols:width + (d + 1) * p_cols])
    up_first = remote(up_send.at[1 - c], up_sib, up_ssem.at[0], up_rsem.at[0], sib)
    up_first.start()

    for distance in range(1, LINE):
        for side in (1, -1):
            @pl.when(on_line(z - side * distance))
            def _():
                take_rows(at(z - side * distance, y, c))

                @pl.when(on_line(z + side))
                def _():
                    line_copy(distance, side).start()

                fan_copy(distance, side, ypart, 1).start()
                fan_copy(distance, side, sib, 2).start()

    up_first.wait()
    up_mid[...] = up_send[c] + up_sib[...]

    reached, cosines, sines = [], [], []
    node = lax.broadcasted_iota(jnp.int32, (tree, tree), 1)
    own = lax.broadcasted_iota(jnp.int32, (tree, tree), 0)
    unit = jnp.where(own == node, 1.0, 0.0).astype(jnp.bfloat16)
    for r in range(requests):
        hot = jnp.where((parents[r:r + 1] == own) | (own == node), 1.0, 0.0)
        hot = lax.dot_general(hot.astype(jnp.bfloat16), unit, (((0,), (0,)), ((), ())),
                              preferred_element_type=jnp.float32)
        for _ in range(tree.bit_length()):
            short = hot.astype(jnp.bfloat16)
            hot = jnp.minimum(
                jnp.dot(short, short, preferred_element_type=jnp.float32), 1.0)
        reached.append(hot)
        depth = jnp.sum(hot, axis=1, keepdims=True).astype(jnp.int32) - 1
        position = (depth + length_of[r]).astype(jnp.float32)
        angles = position * inverse[...]
        cosines.append(jnp.cos(angles))
        sines.append(jnp.sin(angles))

    for k in range(LINE):
        block = at(hop(k), 1 - y, c)
        take_rows(block)
        push_rows(block, sib)

    up_second = remote(up_mid.at[1 - y], up_y, up_ssem.at[1], up_rsem.at[1], ypart)
    up_second.start()

    for k in range(LINE):
        for yy in (y, 1 - y):
            take_rows(at(hop(k), yy, 1 - c))

    half = rows_all.shape[2]

    def norm_step(k, carry):
        parts = []
        for j in range(2):
            block = rows_all[2 * k + j].astype(jnp.float32)
            squares = jnp.sum(block * block, axis=1, keepdims=True)
            scale = lax.rsqrt((squares[:8] + squares[8:]) / (2 * half) + epsilon)
            parts.append((block[:8] * scale, block[8:] * scale))
        for h in range(2):
            both = jnp.concatenate([parts[0][h], parts[1][h]], axis=0)
            cols = slice(h * half, (h + 1) * half)
            normed[pl.ds(pl.multiple_of(k * 16, 16), 16), cols] = (
                both * gain[:, cols]).astype(jnp.bfloat16)
        return carry

    lax.fori_loop(0, count // 2, norm_step, 0)

    nt = (((1,), (1,)), ((), ()))
    tn = (((0,), (0,)), ((), ()))
    loads[1].wait()
    token = lax.broadcasted_iota(jnp.int32, (1, requests * tree), 1)
    low = jnp.zeros((down_here.shape[1], requests * tree), jnp.float32)
    for s in range(slots):
        flag = jnp.where(token < tree, chosen[0][s].astype(jnp.int32),
                         chosen[1][s].astype(jnp.int32))
        value = lax.dot_general(down_here[s], normed[...], nt,
                                preferred_element_type=jnp.float32)
        low = jnp.where(flag == 1, value, low)
    low_send[0] = low.astype(jnp.bfloat16)
    first = remote(low_send.at[0], low_recv.at[0], low_ssem.at[0], low_rsem.at[0], sib)
    first.start()

    up_second.wait()
    up_low[...] = up_mid[y] + up_y[...]
    up_third = []
    for k in range(1, LINE):
        copy = remote(up_low.at[hop(k)], up_z.at[k - 1], up_ssem.at[1 + k], up_rsem.at[1 + k],
                      at(hop(k), y, c))
        copy.start()
        up_third.append(copy)

    loads[2].wait()
    loads[3].wait()
    steps = 4
    depth = w_query.shape[0] // steps
    q_acc = jnp.zeros((requests * tree, q_cols), jnp.float32)
    p_acc = jnp.zeros((requests * tree, p_cols), jnp.float32)
    pending = first
    thirds = []
    for step in range(steps):
        cut = slice(step * depth, (step + 1) * depth)
        q_acc += jnp.dot(normed[:, cut], w_query[cut], preferred_element_type=jnp.float32)
        p_acc += jnp.dot(normed[:, cut], w_pair[cut], preferred_element_type=jnp.float32)
        if step == 0:
            first.wait()
            low_send[1] = low_send[0] + low_recv[0]
            second = remote(low_send.at[1], low_recv.at[1], low_ssem.at[1], low_rsem.at[1], ypart)
            second.start()
        if step == 1:
            second.wait()
            low_send[2] = low_send[1] + low_recv[1]
            for k in range(1, LINE):
                copy = remote(low_send.at[2], low_recv.at[1 + k], low_ssem.at[1 + k],
                              low_rsem.at[1 + k], at(hop(k), y, c))
                copy.start()
                thirds.append(copy)
    for copy in thirds + up_third:
        copy.wait()
    low_all = low_send[2] + low_recv[2] + low_recv[3] + low_recv[4]
    up_all = up_low[z] + up_z[0] + up_z[1] + up_z[2]
    is_value = me >= count // 2
    q_heads = q_cols // 128

    def rotated(vectors, r):
        front, back = vectors[:, :tree], vectors[:, tree:]
        return jnp.concatenate(
            [front * cosines[r] - back * sines[r], back * cosines[r] + front * sines[r]], axis=1)

    for r in range(requests):
        rows = slice(r * tree, (r + 1) * tree)
        low_r = low_all[:, rows]
        up_r = up_all[r * rank:(r + 1) * rank]
        update = lax.dot_general(low_r[:rank], up_r[:, :q_cols], tn,
                                 preferred_element_type=jnp.float32)
        q_pre = (q_acc[rows] + adapter_scale * update).astype(jnp.bfloat16).astype(jnp.float32)
        for h in range(q_heads):
            query_buf[c, r, h] = rotated(q_pre[:, h * 128:(h + 1) * 128], r).astype(jnp.bfloat16)
        pair_low = jnp.where(is_value, low_r[2 * rank:], low_r[rank:2 * rank])
        update = lax.dot_general(pair_low, up_r[:, q_cols:], tn,
                                 preferred_element_type=jnp.float32)
        p_pre = (p_acc[rows] + adapter_scale * update).astype(jnp.bfloat16).astype(jnp.float32)
        final = jnp.where(is_value, p_pre, rotated(p_pre, r)).astype(jnp.bfloat16)
        for m in range(CORES):
            pair_own[m, r] = final[m * (tree // 2):(m + 1) * (tree // 2)]

    q_copy = remote(query_buf.at[c], query_buf.at[c], query_sem.at[0], query_sem.at[1], sib)
    q_copy.start()
    group = me % (count // 2)
    for is_v, landing in ((0, tree_keys), (1, tree_values)):
        for m in range(CORES):
            target = group * CORES + m

            @pl.when((is_value == (is_v == 1)) & (target != me))
            def _():
                remote(pair_own.at[m], landing, pair_ssem.at[m], pair_rsem.at[is_v], target).start()

            @pl.when((is_value == (is_v == 1)) & (target == me))
            def _():
                landing[...] = pair_own[m]

    for m in range(CORES):
        @pl.when(group * CORES + m != me)
        def _():
            remote(pair_own.at[m], tree_keys, pair_ssem.at[m], pair_rsem.at[0], sib).wait_send()

    @pl.when(me // CORES != me)
    def _():
        remote(pair_own.at[0], tree_keys, pair_ssem.at[0], pair_rsem.at[0], sib).wait_recv()

    @pl.when(me // CORES + count // 2 != me)
    def _():
        remote(pair_own.at[0], tree_values, pair_ssem.at[0], pair_rsem.at[1], sib).wait_recv()

    q_copy.wait_send()
    remote(query_buf.at[1 - c], query_buf.at[1 - c], query_sem.at[0], query_sem.at[1],
           sib).wait_recv()

    loads[4].wait()
    heads = CORES * q_heads
    block_rows = heads * tree
    scale = 128 ** -0.5
    slots_here = kv_cache.shape[2]
    for r in range(requests):
        queries = query_buf[:, r].reshape(block_rows, 128)
        mask = jnp.where(c == 0, reached[r][:, :tree // 2], reached[r][:, tree // 2:])
        mask = jnp.concatenate([mask] * heads, axis=0)
        scores = lax.dot_general(queries, tree_keys[r], nt,
                                 preferred_element_type=jnp.float32) * scale
        scores = jnp.where(mask > 0.5, scores, masked_score)
        top = jnp.maximum(jnp.max(scores, axis=1, keepdims=True), lowest)
        weights = jnp.exp(scores - top)
        total = jnp.sum(weights, axis=1, keepdims=True)
        blend = jnp.dot(weights.astype(jnp.bfloat16), tree_values[r],
                        preferred_element_type=jnp.float32)
        limit = length_of[r] - c * slots_here

        def key_step(j, carry):
            top, total, blend = carry
            start = pl.multiple_of(j * KEY_CHUNK, KEY_CHUNK)
            scores = lax.dot_general(queries, kv_cache[0, r, pl.ds(start, KEY_CHUNK)], nt,
                                     preferred_element_type=jnp.float32) * scale
            column = lax.broadcasted_iota(jnp.int32, (1, KEY_CHUNK), 1) + start
            scores = jnp.where(column < limit, scores, masked_score)
            new_top = jnp.maximum(top, jnp.max(scores, axis=1, keepdims=True))
            weights = jnp.exp(scores - new_top)
            factor = jnp.exp(top - new_top)
            total = total * factor + jnp.sum(weights, axis=1, keepdims=True)
            blend = blend * factor + jnp.dot(
                weights.astype(jnp.bfloat16), kv_cache[1, r, pl.ds(start, KEY_CHUNK)],
                preferred_element_type=jnp.float32)
            return new_top, total, blend

        top, total, blend = lax.fori_loop(0, slots_here // KEY_CHUNK, key_step,
                                          (top, total, blend))
        top = jnp.broadcast_to(top, blend.shape)
        total = jnp.broadcast_to(total, blend.shape)
        mine = block_rows // CORES
        for m in range(CORES):
            cut = slice(m * mine, (m + 1) * mine)
            merge_send[m, r, 0] = blend[cut]
            merge_send[m, r, 1] = top[cut]
            merge_send[m, r, 2] = total[cut]
        remote(merge_send.at[1 - c, r], merge_recv.at[r], merge_ssem.at[r], merge_rsem.at[r],
               sib).start()

    loads[5].wait()
    for r in range(requests):
        remote(merge_send.at[1 - c, r], merge_recv.at[r], merge_ssem.at[r], merge_rsem.at[r],
               sib).wait()
        top = jnp.maximum(merge_send[c, r, 1], merge_recv[r, 1])
        f_own, f_other = jnp.exp(merge_send[c, r, 1] - top), jnp.exp(merge_recv[r, 1] - top)
        total = merge_send[c, r, 2] * f_own + merge_recv[r, 2] * f_other
        value = (merge_send[c, r, 0] * f_own + merge_recv[r, 0] * f_other) / total
        value = value.astype(jnp.bfloat16)
        for h in range(q_heads):
            attention[r * tree:(r + 1) * tree, h * 128:(h + 1) * 128] = (
                value[h * tree:(h + 1) * tree])

    columns = w_out.shape[1] // OUT_CHUNKS

    def sib_copy(n):
        return remote(part.at[n, 1 - c], part_sib.at[n], sib_ssem.at[n], sib_rsem.at[n], sib)

    def y_copy(n):
        return remote(y_send.at[n], y_recv.at[n], y_ssem.at[n], y_rsem.at[n], ypart)

    def z_copy(n, k):
        return remote(z_send.at[n, hop(k)], z_recv.at[n, k - 1], z_ssem.at[n, k - 1],
                      z_rsem.at[n, k - 1], at(hop(k), y, c))

    def project(n):
        product = jnp.dot(attention[...], w_out[:, n * columns:(n + 1) * columns],
                          preferred_element_type=jnp.float32)
        for d in range(count):
            part[n, d % 2, d // 2 % 2, d // 4] = product[d * 8:(d + 1) * 8]
        sib_copy(n).start()

    def sum_pair(n):
        sib_copy(n).wait()
        away = part[n, c, 1 - y] + part_sib[n, 1 - y]
        y_send[n] = away.reshape(LINE * 8, columns).astype(jnp.bfloat16)
        y_copy(n).start()

    def sum_y(n):
        y_copy(n).wait()
        held = (part[n, c, y] + part_sib[n, y]) + y_recv[n].astype(jnp.float32).reshape(
            LINE, 8, columns)
        part_sib[n, 0] = held
        for d in range(LINE):
            z_send[n, d] = jnp.concatenate(
                [held[d, :, :columns // 2], held[d, :, columns // 2:]], axis=0).astype(jnp.bfloat16)
        for k in range(1, LINE):
            z_copy(n, k).start()

    for turn in range(OUT_CHUNKS + 2):
        if turn < OUT_CHUNKS:
            project(turn)
        if 1 <= turn <= OUT_CHUNKS:
            sum_pair(turn - 1)
        if turn >= 2:
            sum_y(turn - 2)
    for n in range(OUT_CHUNKS):
        total = part_sib[n, 0, z]
        for k in range(1, LINE):
            z_copy(n, k).wait()
            landed = z_recv[n, k - 1].astype(jnp.float32)
            total = total + jnp.concatenate([landed[:8], landed[8:]], axis=1)
        out[:, n * columns:(n + 1) * columns] = total.astype(jnp.bfloat16)

    for copy in sent:
        copy.wait_send()
    for distance in range(LINE):
        for side in (1, -1):
            @pl.when(on_line(z - side * distance) & on_line(z + side))
            def _():
                line_copy(distance, side).wait_send()

            if distance > 0:
                @pl.when(on_line(z - side * distance))
                def _():
                    fan_copy(distance, side, ypart, 1).wait_send()
                    fan_copy(distance, side, sib, 2).wait_send()


def fused_body(
    layer_input, input_norm_gain, query_weight, key_value_weight, output_weight,
    cached_key_value, adapter_down_weight, adapter_up_weight, request_adapter,
    adapter_storage_index, cached_length, parent_node,
):
    rows, model = layer_input.shape
    half = model // 2
    packed = layer_input.reshape(rows, 2, half).transpose(1, 0, 2).reshape(2 * rows, half)
    exponents = np.arange(64) * (2.0 / 128)
    inverse = jnp.asarray(np.exp(exponents * -math.log(rope_base))[None].astype(np.float32))
    bf, f32 = jnp.bfloat16, jnp.float32
    count = 16
    rank = adapter_up_weight.shape[1]
    ranks = adapter_down_weight.shape[1]
    cols = query_weight.shape[1] + key_value_weight.shape[1]
    columns = model // OUT_CHUNKS
    dma = pltpu.SemaphoreType.DMA
    n = OUT_CHUNKS
    scratch = [
        pltpu.VMEM(query_weight.shape, bf), pltpu.VMEM(key_value_weight.shape, bf),
        pltpu.VMEM(output_weight.shape, bf), pltpu.VMEM(cached_key_value.shape, bf),
        pltpu.VMEM((count, 2 * rows, half), bf), pltpu.VMEM((count * rows, model), bf),
        pltpu.VMEM(adapter_down_weight.shape, bf), pltpu.VMEM(adapter_up_weight.shape, bf),
        pltpu.VMEM((2, 2, 4, 2 * rank, cols), bf), pltpu.VMEM((2, 4, 2 * rank, cols), bf),
        pltpu.VMEM((2, 4, 2 * rank, cols), bf), pltpu.VMEM((4, 2 * rank, cols), bf),
        pltpu.VMEM((4, 2 * rank, cols), bf), pltpu.VMEM((3, 2 * rank, cols), bf),
        pltpu.VMEM((3, ranks, 128), bf), pltpu.VMEM((5, ranks, 128), bf),
        pltpu.VMEM((2, 2, 4, 64, 128), bf), pltpu.VMEM((2, 2, 32, 128), bf),
        pltpu.VMEM((2, 32, 128), bf), pltpu.VMEM((2, 32, 128), bf),
        pltpu.VMEM((2, 2, 3, 256, 128), f32), pltpu.VMEM((2, 3, 256, 128), f32),
        pltpu.VMEM((128, 512), bf),
        pltpu.VMEM((n, 2, 2, 4, 8, columns), f32), pltpu.VMEM((n, 2, 4, 8, columns), f32),
        pltpu.VMEM((n, 32, columns), bf), pltpu.VMEM((n, 32, columns), bf),
        pltpu.VMEM((n, 4, 16, columns // 2), bf), pltpu.VMEM((n, 3, 16, columns // 2), bf),
        dma((6,)), dma((6,)), dma((4, 2, 3)), dma((count,)), dma((5,)), dma((5,)), dma((5,)), dma((5,)),
        dma((2,)), dma((2,)), dma((2,)), dma((2,)), dma((2,)),
        dma((n,)), dma((n,)), dma((n,)), dma((n,)), dma((n, 3)), dma((n, 3)),
    ]
    smem = pl.BlockSpec(memory_space=pltpu.SMEM)
    vmem = pl.BlockSpec(memory_space=pltpu.VMEM)
    hbm = pl.BlockSpec(memory_space=pl.ANY)
    return pl.pallas_call(
        fused_kernel,
        out_shape=jax.ShapeDtypeStruct((rows, model), bf),
        in_specs=[smem] * 3 + [vmem] * 4 + [hbm] * 6,
        out_specs=vmem,
        scratch_shapes=scratch,
        compiler_params=pltpu.CompilerParams(
            collective_id=0, has_side_effects=True, vmem_limit_bytes=60 * 2**20),
        cost_estimate=pl.CostEstimate(
            flops=5 * 10**9, bytes_accessed=25 * 2**20, transcendentals=4 * 2**20),
        name="fused_layer",
    )(adapter_storage_index, request_adapter, cached_length, packed, input_norm_gain[None],
      parent_node, inverse, adapter_down_weight, adapter_up_weight,
      query_weight, key_value_weight, output_weight, cached_key_value)


def solution(mesh):
    in_specs = (
        P(("rep", "tp"), None),
        P(),
        P(None, "tp"),
        P(None, "tp"),
        P("tp", None),
        P(None, "rep", "tp", None),
        P("tp", None, None),
        P("tp", None, None),
        P("rep"),
        P(),
        P("rep"),
        P("rep", None),
    )
    out_specs = P(("rep", "tp"), None)
    fused = mesh.shape["tp"] == 16 and mesh.shape["rep"] == 2
    return jax.shard_map(fused_body if fused else body, mesh=mesh, in_specs=in_specs, out_specs=out_specs, check_vma=False)
```

```python
import math

import jax
import numpy as np
import jax.numpy as jnp
from jax import lax
from jax.experimental import pallas as pl
from jax.experimental.pallas import tpu as pltpu
from jax.sharding import PartitionSpec as P

KEY_HEADS = 8


epsilon = 1e-05
adapter_scale = 0.5
rope_base = 500000.0
masked_score = -1e30


def broadcast(block, axis, source):
    block = jnp.where(lax.axis_index(axis) == source, block, jnp.zeros_like(block))
    return lax.psum(block, axis)


def partner_2(value, axis, stride):
    mask = 2**stride
    pairs = [(source, source ^ mask) for source in range(lax.axis_size(axis))]
    return lax.ppermute(value, axis, pairs)


def for_sending(x):

    def short(part):
        return part.astype(jnp.bfloat16) if part.dtype == jnp.float32 else part

    return jax.tree.map(short, x)


def normalize(hidden_rows, input_norm_gain):
    widened = hidden_rows.astype(jnp.float32)
    squares_mean = jnp.mean(widened * widened, axis=-1, keepdims=True)
    return (widened * lax.rsqrt(squares_mean + epsilon) * input_norm_gain).astype(jnp.bfloat16)


def ancestors(parents):
    node_count = parents.shape[0]
    node_index = jnp.arange(node_count, dtype=jnp.int32)
    parent_hot = (parents[:, None] == node_index[None, :]).astype(jnp.float32)
    reached = jnp.maximum(parent_hot, jnp.eye(node_count, dtype=jnp.float32))
    for repeat in range(node_count.bit_length()):
        reached = jnp.minimum(jnp.dot(reached, reached, precision=lax.Precision.HIGHEST), 1.0)
    return reached


def rotate(vectors, positions):
    half_dim = vectors.shape[-1] // 2
    exponents = jnp.arange(half_dim, dtype=jnp.float32) * (2.0 / vectors.shape[-1])
    inverse = jnp.exp(exponents * -math.log(rope_base))
    angles = positions.astype(jnp.float32)[:, None, None] * inverse[None, None, :]
    cosine = jnp.cos(angles)
    sine_part = jnp.sin(angles)
    leading = vectors[..., :half_dim]
    second = vectors[..., half_dim:]
    return jnp.concatenate(
        [leading * cosine - second * sine_part, second * cosine + leading * sine_part], axis=-1
    )


def project_down(tree_token_rows, down_result):
    return lax.dot_general(
        tree_token_rows, down_result, (((1,), (1,)), ((), ())), preferred_element_type=jnp.float32
    ).astype(jnp.bfloat16)


def spread(per_head, offset, width, head_dim):
    expanded = jnp.repeat(per_head, head_dim, axis=1)
    return lax.dynamic_slice_in_dim(expanded, offset, width, 1)


def combine(own_state, other_state, offset, head_dim):
    width = own_state[0].shape[1]
    new_top = jnp.maximum(own_state[1], other_state[1])
    own_factor = jnp.exp(own_state[1] - new_top)
    other_factor = jnp.exp(other_state[1] - new_top)
    new_total = own_state[2] * own_factor + other_state[2] * other_factor
    new_values = own_state[0] * spread(own_factor, offset, width, head_dim) + other_state[
        0
    ] * spread(other_factor, offset, width, head_dim)
    return (new_values, new_top, new_total)


def partial_attention(queries, all_keys, all_values, usable, group_heads):
    scores = lax.dot_general(
        queries, all_keys, (((1,), (1,)), ((), ())), preferred_element_type=jnp.float32
    ) * all_keys.shape[1] ** (-0.5)
    mask_rows = jnp.repeat(usable, group_heads, axis=0)
    scores = jnp.where(mask_rows, scores, masked_score)
    row_top = jnp.max(scores, axis=1, keepdims=True)
    weights = jnp.where(mask_rows, jnp.exp(scores - row_top), 0.0)
    row_total = jnp.sum(weights, axis=1, keepdims=True)
    blended = jnp.dot(weights.astype(jnp.bfloat16), all_values, preferred_element_type=jnp.float32)
    return (blended, row_top, row_total)


def body(
    layer_input,
    input_norm_gain,
    query_weight,
    key_value_weight,
    output_weight,
    cached_key_value,
    adapter_down_weight,
    adapter_up_weight,
    request_adapter,
    adapter_storage_index,
    cached_length,
    parent_node,
):
    devices = lax.axis_size("tp")
    device = lax.axis_index("tp")
    model_dim = query_weight.shape[0]
    query_cols = query_weight.shape[1]
    pair_cols = key_value_weight.shape[1]
    storage_slot_list = adapter_down_weight.shape[0]
    total_rank = adapter_down_weight.shape[1]
    rank_size = total_rank // 3
    requests = request_adapter.shape[0]
    tree_size = parent_node.shape[1]
    head_dim = cached_key_value.shape[3]
    block_keys = cached_key_value.shape[2]
    kv_width = pair_cols * devices // 2
    group_size = devices // KEY_HEADS
    depth_levels = group_size.bit_length() - 1
    head_group = device // group_size
    member = device % group_size
    group_width = query_cols * group_size
    group_heads = group_width // head_dim
    tree_block = tree_size // group_size
    everyone = lax.all_gather(layer_input, "tp", axis=0, tiled=True)
    normed = normalize(everyone, input_norm_gain)
    kv_start = device * pair_cols
    is_value = kv_start >= kv_width
    query_blocks = []
    pair_blocks = []
    for request in range(requests):
        storage_slot_index = adapter_storage_index[request_adapter[request]]
        owner_index = storage_slot_index // storage_slot_list
        slot_local = storage_slot_index % storage_slot_list
        request_down = lax.dynamic_index_in_dim(adapter_down_weight, slot_local, 0, keepdims=False)
        request_up = lax.dynamic_index_in_dim(adapter_up_weight, slot_local, 0, keepdims=False)
        tree_token_rows = normed[request * tree_size : (request + 1) * tree_size]
        down_result, up_result = (
            broadcast(request_down, "tp", owner_index),
            broadcast(request_up, "tp", owner_index),
        )
        low_rank = project_down(tree_token_rows, down_result)
        query_update = jnp.dot(
            low_rank[:, :rank_size],
            lax.dynamic_slice_in_dim(up_result, device * query_cols, query_cols, 1),
            preferred_element_type=jnp.float32,
        )
        query_blocks.append(
            (
                jnp.dot(tree_token_rows, query_weight, preferred_element_type=jnp.float32)
                + adapter_scale * query_update
            ).astype(jnp.bfloat16)
        )
        pair_rank = jnp.where(
            is_value, low_rank[:, 2 * rank_size :], low_rank[:, rank_size : 2 * rank_size]
        )
        paired_update = jnp.dot(
            pair_rank,
            lax.dynamic_slice_in_dim(up_result, model_dim + kv_start, pair_cols, 1),
            preferred_element_type=jnp.float32,
        )
        pair_blocks.append(
            (
                jnp.dot(tree_token_rows, key_value_weight, preferred_element_type=jnp.float32)
                + adapter_scale * paired_update
            ).astype(jnp.bfloat16)
        )
    query_local = jnp.concatenate(query_blocks, axis=0)
    pair_local = jnp.concatenate(pair_blocks, axis=0)
    pair_all = lax.all_gather(pair_local, "tp", axis=1, tiled=True)
    query_group = query_local
    for section_bit in range(depth_levels):
        partner = partner_2(query_group, "tp", section_bit)
        upper_half = member // 2**section_bit % 2 == 1
        query_group = jnp.concatenate(
            [
                jnp.where(upper_half, partner, query_group),
                jnp.where(upper_half, query_group, partner),
            ],
            axis=1,
        )
    key_cols = lax.dynamic_slice_in_dim(pair_all, head_group * head_dim, head_dim, 1)
    value_cols = lax.dynamic_slice_in_dim(pair_all, kv_width + head_group * head_dim, head_dim, 1)
    block_index = member * block_keys + jnp.arange(block_keys, dtype=jnp.int32)
    value_parts = []
    top_parts = []
    total_parts = []
    for request in range(requests):
        reached = ancestors(parent_node[request])
        node_depth = jnp.sum(reached, axis=1).astype(jnp.int32) - 1
        positions = cached_length[request] + node_depth
        request_queries = query_group[request * tree_size : (request + 1) * tree_size]
        queries = (
            rotate(
                request_queries.astype(jnp.float32).reshape(tree_size, group_heads, head_dim),
                positions,
            )
            .astype(jnp.bfloat16)
            .reshape(tree_size * group_heads, head_dim)
        )
        request_keys = key_cols[request * tree_size : (request + 1) * tree_size]
        new_keys = (
            rotate(request_keys.astype(jnp.float32).reshape(tree_size, 1, head_dim), positions)
            .astype(jnp.bfloat16)
            .reshape(tree_size, head_dim)
        )
        tree_keys = lax.dynamic_slice_in_dim(new_keys, member * tree_block, tree_block, 0)
        tree_values = lax.dynamic_slice_in_dim(
            value_cols[request * tree_size : (request + 1) * tree_size],
            member * tree_block,
            tree_block,
            0,
        )
        tree_mask = lax.dynamic_slice_in_dim(reached, member * tree_block, tree_block, 1) > 0.5
        cache_mask = jnp.broadcast_to(
            (block_index < cached_length[request])[None, :], (tree_size, block_keys)
        )
        all_keys = jnp.concatenate([cached_key_value[0, request], tree_keys], axis=0)
        all_values = jnp.concatenate([cached_key_value[1, request], tree_values], axis=0)
        blended, row_top, row_total = partial_attention(
            queries,
            all_keys,
            all_values,
            jnp.concatenate([cache_mask, tree_mask], axis=1),
            group_heads,
        )
        value_parts.append(blended.reshape(tree_size, group_width))
        top_parts.append(row_top.reshape(tree_size, group_heads))
        total_parts.append(row_total.reshape(tree_size, group_heads))
    merged = (
        jnp.concatenate(value_parts, axis=0),
        jnp.concatenate(top_parts, axis=0),
        jnp.concatenate(total_parts, axis=0),
    )
    window = group_width // group_size
    zero_offset = jnp.zeros((), jnp.int32)
    for section_bit in range(depth_levels):
        other_state = partner_2(
            (for_sending(merged[0]), for_sending(merged[1]), for_sending(merged[2])),
            "tp",
            section_bit,
        )
        merged = combine(merged, other_state, zero_offset, head_dim)
    offset = member * window
    kept_values = lax.dynamic_slice_in_dim(merged[0], offset, window, 1)
    attention = (kept_values / spread(merged[2], offset, window, head_dim)).astype(jnp.bfloat16)
    summed = lax.psum_scatter(
        jnp.dot(attention, output_weight, preferred_element_type=jnp.float32),
        "tp",
        scatter_dimension=0,
        tiled=True,
    )
    return summed.astype(jnp.bfloat16)


MESH = pl.DeviceIdType.MESH
LINE, PAIR, CORES = 4, 2, 2
OUT_CHUNKS = 4
KEY_CHUNK = 1024
lowest = -1e29


def fused_kernel(
    slot_of, adapter_of, length_of, rows_in, gain, parents, inverse, down, up,
    query_weight, pair_weight, out_weight, cache, out,
    w_query, w_pair, w_out, kv_cache, rows_all, normed, down_here, up_here,
    up_send, up_sib, up_mid, up_y, up_low, up_z, low_send, low_recv,
    query_buf, pair_own, tree_keys, tree_values,
    merge_send, merge_recv, attention, part, part_sib, y_send, y_recv, z_send, z_recv,
    load_sem, rows_send, line_send, rows_recv, up_ssem, up_rsem, low_ssem, low_rsem,
    query_sem, pair_ssem, pair_rsem, merge_ssem, merge_rsem,
    sib_ssem, sib_rsem, y_ssem, y_rsem, z_ssem, z_rsem,
):
    me = lax.axis_index("tp")
    z, y, c = me // (PAIR * CORES), me // CORES % PAIR, me % CORES
    count = LINE * PAIR * CORES

    def at(zz, yy, cc):
        return (zz * PAIR + yy) * CORES + cc

    def hop(k):
        return (z + k) % LINE

    def remote(src, dst, ssem, rsem, target):
        return pltpu.make_async_remote_copy(
            src_ref=src, dst_ref=dst, send_sem=ssem, recv_sem=rsem,
            device_id={"tp": target}, device_id_type=MESH,
        )

    sib, ypart = at(z, y, 1 - c), at(z, 1 - y, c)
    loads = [
        pltpu.make_async_copy(a, b, load_sem.at[i])
        for i, (a, b) in enumerate([
            (up, up_here), (down, down_here), (query_weight, w_query),
            (pair_weight, w_pair), (cache, kv_cache), (out_weight, w_out)])
    ]
    for load in loads:
        load.start()
    barrier = pltpu.get_barrier_semaphore()
    for k in range(1, count):
        pl.semaphore_signal(
            barrier, inc=1, device_id={"tp": (me + k) % count}, device_id_type=MESH)
    rows_all[me] = rows_in[...]
    pl.semaphore_wait(barrier, count - 1)

    sent = []

    def push_rows(block, target):
        copy = remote(rows_all.at[block], rows_all.at[block],
                      rows_send.at[len(sent)], rows_recv.at[block], target)
        copy.start()
        sent.append(copy)

    def take_rows(block):
        remote(rows_all.at[block], rows_all.at[block], rows_send.at[0],
               rows_recv.at[block], sib).wait_recv()

    def line_copy(distance, side):
        block = at(z - side * distance, y, c)
        return remote(rows_all.at[block], rows_all.at[block],
                      line_send.at[distance, (side + 1) // 2, 0], rows_recv.at[block],
                      at(z + side, y, c))

    def fan_copy(distance, side, target, place):
        block = at(z - side * distance, y, c)
        return remote(rows_all.at[block], rows_all.at[block],
                      line_send.at[distance, (side + 1) // 2, place], rows_recv.at[block], target)

    def on_line(place):
        return (place >= 0) & (place < LINE)

    for side in (1, -1):
        @pl.when(on_line(z + side))
        def _():
            line_copy(0, side).start()
    push_rows(me, ypart)
    push_rows(me, sib)

    requests, tree = 2, 64
    rank, slots = up_here.shape[1], up_here.shape[0]
    q_cols, p_cols = w_query.shape[1], w_pair.shape[1]
    width = q_cols * count
    chosen = []
    for r in range(requests):
        slot = slot_of[adapter_of[r]]
        chosen.append([slot == me * slots + s for s in range(slots)])
    loads[0].wait()
    for r in range(requests):
        picked = jnp.zeros(up_here.shape[1:], up_here.dtype)
        for s in range(slots):
            picked = jnp.where(chosen[r][s], up_here[s], picked)
        for d in range(count):
            zz, yy, cc = d // 4, d // 2 % 2, d % 2
            up_send[cc, yy, zz, r * rank:(r + 1) * rank, :q_cols] = (
                picked[:, d * q_cols:(d + 1) * q_cols])
            up_send[cc, yy, zz, r * rank:(r + 1) * rank, q_cols:] = (
                picked[:, width + d * p_cols:width + (d + 1) * p_cols])
    up_first = remote(up_send.at[1 - c], up_sib, up_ssem.at[0], up_rsem.at[0], sib)
    up_first.start()

    for distance in range(1, LINE):
        for side in (1, -1):
            @pl.when(on_line(z - side * distance))
            def _():
                take_rows(at(z - side * distance, y, c))

                @pl.when(on_line(z + side))
                def _():
                    line_copy(distance, side).start()

                fan_copy(distance, side, ypart, 1).start()
                fan_copy(distance, side, sib, 2).start()

    up_first.wait()
    up_mid[...] = up_send[c] + up_sib[...]

    reached, cosines, sines = [], [], []
    node = lax.broadcasted_iota(jnp.int32, (tree, tree), 1)
    own = lax.broadcasted_iota(jnp.int32, (tree, tree), 0)
    unit = jnp.where(own == node, 1.0, 0.0).astype(jnp.bfloat16)
    for r in range(requests):
        hot = jnp.where((parents[r:r + 1] == own) | (own == node), 1.0, 0.0)
        hot = lax.dot_general(hot.astype(jnp.bfloat16), unit, (((0,), (0,)), ((), ())),
                              preferred_element_type=jnp.float32)
        for _ in range(tree.bit_length()):
            short = hot.astype(jnp.bfloat16)
            hot = jnp.minimum(
                jnp.dot(short, short, preferred_element_type=jnp.float32), 1.0)
        reached.append(hot)
        depth = jnp.sum(hot, axis=1, keepdims=True).astype(jnp.int32) - 1
        position = (depth + length_of[r]).astype(jnp.float32)
        angles = position * inverse[...]
        cosines.append(jnp.cos(angles))
        sines.append(jnp.sin(angles))

    half = rows_all.shape[2]

    def norm_chip(k):
        parts = []
        for j in range(2):
            block = rows_all[2 * k + j].astype(jnp.float32)
            squares = jnp.sum(block * block, axis=1, keepdims=True)
            scale = lax.rsqrt((squares[:8] + squares[8:]) / (2 * half) + epsilon)
            parts.append((block[:8] * scale, block[8:] * scale))
        for h in range(2):
            both = jnp.concatenate([parts[0][h], parts[1][h]], axis=0)
            cols = slice(h * half, (h + 1) * half)
            normed[pl.ds(pl.multiple_of(k * 16, 16), 16), cols] = (
                both * gain[:, cols]).astype(jnp.bfloat16)

    for k in range(LINE):
        block = at(hop(k), 1 - y, c)
        take_rows(block)
        push_rows(block, sib)
        take_rows(at(hop(k), y, 1 - c))
        norm_chip(hop(k) * PAIR + y)

    up_second = remote(up_mid.at[1 - y], up_y, up_ssem.at[1], up_rsem.at[1], ypart)
    up_second.start()

    for k in range(LINE):
        take_rows(at(hop(k), 1 - y, 1 - c))
        norm_chip(hop(k) * PAIR + 1 - y)

    nt = (((1,), (1,)), ((), ()))
    tn = (((0,), (0,)), ((), ()))
    loads[1].wait()
    token = lax.broadcasted_iota(jnp.int32, (1, requests * tree), 1)
    low = jnp.zeros((down_here.shape[1], requests * tree), jnp.float32)
    for s in range(slots):
        flag = jnp.where(token < tree, chosen[0][s].astype(jnp.int32),
                         chosen[1][s].astype(jnp.int32))
        value = lax.dot_general(down_here[s], normed[...], nt,
                                preferred_element_type=jnp.float32)
        low = jnp.where(flag == 1, value, low)
    low_send[0] = low.astype(jnp.bfloat16)
    first = remote(low_send.at[0], low_recv.at[0], low_ssem.at[0], low_rsem.at[0], sib)
    first.start()

    up_second.wait()
    up_low[...] = up_mid[y] + up_y[...]
    up_third = []
    for k in range(1, LINE):
        copy = remote(up_low.at[hop(k)], up_z.at[k - 1], up_ssem.at[1 + k], up_rsem.at[1 + k],
                      at(hop(k), y, c))
        copy.start()
        up_third.append(copy)

    loads[2].wait()
    loads[3].wait()
    steps = 4
    depth = w_query.shape[0] // steps
    q_acc = jnp.zeros((requests * tree, q_cols), jnp.float32)
    p_acc = jnp.zeros((requests * tree, p_cols), jnp.float32)
    pending = first
    thirds = []
    for step in range(steps):
        cut = slice(step * depth, (step + 1) * depth)
        q_acc += jnp.dot(normed[:, cut], w_query[cut], preferred_element_type=jnp.float32)
        p_acc += jnp.dot(normed[:, cut], w_pair[cut], preferred_element_type=jnp.float32)
        if step == 0:
            first.wait()
            low_send[1] = low_send[0] + low_recv[0]
            second = remote(low_send.at[1], low_recv.at[1], low_ssem.at[1], low_rsem.at[1], ypart)
            second.start()
        if step == 1:
            second.wait()
            low_send[2] = low_send[1] + low_recv[1]
            for k in range(1, LINE):
                copy = remote(low_send.at[2], low_recv.at[1 + k], low_ssem.at[1 + k],
                              low_rsem.at[1 + k], at(hop(k), y, c))
                copy.start()
                thirds.append(copy)
    for copy in thirds + up_third:
        copy.wait()
    low_all = low_send[2] + low_recv[2] + low_recv[3] + low_recv[4]
    up_all = up_low[z] + up_z[0] + up_z[1] + up_z[2]
    is_value = me >= count // 2
    q_heads = q_cols // 128

    def rotated(vectors, r):
        front, back = vectors[:, :tree], vectors[:, tree:]
        return jnp.concatenate(
            [front * cosines[r] - back * sines[r], back * cosines[r] + front * sines[r]], axis=1)

    for r in range(requests):
        rows = slice(r * tree, (r + 1) * tree)
        low_r = low_all[:, rows]
        up_r = up_all[r * rank:(r + 1) * rank]
        update = lax.dot_general(low_r[:rank], up_r[:, :q_cols], tn,
                                 preferred_element_type=jnp.float32)
        q_pre = (q_acc[rows] + adapter_scale * update).astype(jnp.bfloat16).astype(jnp.float32)
        for h in range(q_heads):
            query_buf[c, r, h] = rotated(q_pre[:, h * 128:(h + 1) * 128], r).astype(jnp.bfloat16)
        pair_low = jnp.where(is_value, low_r[2 * rank:], low_r[rank:2 * rank])
        update = lax.dot_general(pair_low, up_r[:, q_cols:], tn,
                                 preferred_element_type=jnp.float32)
        p_pre = (p_acc[rows] + adapter_scale * update).astype(jnp.bfloat16).astype(jnp.float32)
        final = jnp.where(is_value, p_pre, rotated(p_pre, r)).astype(jnp.bfloat16)
        for m in range(CORES):
            pair_own[m, r] = final[m * (tree // 2):(m + 1) * (tree // 2)]

    q_copy = remote(query_buf.at[c], query_buf.at[c], query_sem.at[0], query_sem.at[1], sib)
    q_copy.start()
    group = me % (count // 2)
    for is_v, landing in ((0, tree_keys), (1, tree_values)):
        for m in range(CORES):
            target = group * CORES + m

            @pl.when((is_value == (is_v == 1)) & (target != me))
            def _():
                remote(pair_own.at[m], landing, pair_ssem.at[m], pair_rsem.at[is_v], target).start()

            @pl.when((is_value == (is_v == 1)) & (target == me))
            def _():
                landing[...] = pair_own[m]

    for m in range(CORES):
        @pl.when(group * CORES + m != me)
        def _():
            remote(pair_own.at[m], tree_keys, pair_ssem.at[m], pair_rsem.at[0], sib).wait_send()

    @pl.when(me // CORES != me)
    def _():
        remote(pair_own.at[0], tree_keys, pair_ssem.at[0], pair_rsem.at[0], sib).wait_recv()

    @pl.when(me // CORES + count // 2 != me)
    def _():
        remote(pair_own.at[0], tree_values, pair_ssem.at[0], pair_rsem.at[1], sib).wait_recv()

    q_copy.wait_send()
    remote(query_buf.at[1 - c], query_buf.at[1 - c], query_sem.at[0], query_sem.at[1],
           sib).wait_recv()

    loads[4].wait()
    heads = CORES * q_heads
    block_rows = heads * tree
    scale = 128 ** -0.5
    slots_here = kv_cache.shape[2]
    for r in range(requests):
        queries = query_buf[:, r].reshape(block_rows, 128)
        mask = jnp.where(c == 0, reached[r][:, :tree // 2], reached[r][:, tree // 2:])
        mask = jnp.concatenate([mask] * heads, axis=0)
        scores = lax.dot_general(queries, tree_keys[r], nt,
                                 preferred_element_type=jnp.float32) * scale
        scores = jnp.where(mask > 0.5, scores, masked_score)
        top = jnp.maximum(jnp.max(scores, axis=1, keepdims=True), lowest)
        weights = jnp.exp(scores - top)
        total = jnp.sum(weights, axis=1, keepdims=True)
        blend = jnp.dot(weights.astype(jnp.bfloat16), tree_values[r],
                        preferred_element_type=jnp.float32)
        limit = length_of[r] - c * slots_here

        def key_step(j, carry):
            top, total, blend = carry
            start = pl.multiple_of(j * KEY_CHUNK, KEY_CHUNK)
            scores = lax.dot_general(queries, kv_cache[0, r, pl.ds(start, KEY_CHUNK)], nt,
                                     preferred_element_type=jnp.float32) * scale
            column = lax.broadcasted_iota(jnp.int32, (1, KEY_CHUNK), 1) + start
            scores = jnp.where(column < limit, scores, masked_score)
            new_top = jnp.maximum(top, jnp.max(scores, axis=1, keepdims=True))
            weights = jnp.exp(scores - new_top)
            factor = jnp.exp(top - new_top)
            total = total * factor + jnp.sum(weights, axis=1, keepdims=True)
            blend = blend * factor + jnp.dot(
                weights.astype(jnp.bfloat16), kv_cache[1, r, pl.ds(start, KEY_CHUNK)],
                preferred_element_type=jnp.float32)
            return new_top, total, blend

        top, total, blend = lax.fori_loop(0, slots_here // KEY_CHUNK, key_step,
                                          (top, total, blend))
        top = jnp.broadcast_to(top, blend.shape)
        total = jnp.broadcast_to(total, blend.shape)
        mine = block_rows // CORES
        for m in range(CORES):
            cut = slice(m * mine, (m + 1) * mine)
            merge_send[m, r, 0] = blend[cut]
            merge_send[m, r, 1] = top[cut]
            merge_send[m, r, 2] = total[cut]
        remote(merge_send.at[1 - c, r], merge_recv.at[r], merge_ssem.at[r], merge_rsem.at[r],
               sib).start()

    loads[5].wait()
    for r in range(requests):
        remote(merge_send.at[1 - c, r], merge_recv.at[r], merge_ssem.at[r], merge_rsem.at[r],
               sib).wait()
        top = jnp.maximum(merge_send[c, r, 1], merge_recv[r, 1])
        f_own, f_other = jnp.exp(merge_send[c, r, 1] - top), jnp.exp(merge_recv[r, 1] - top)
        total = merge_send[c, r, 2] * f_own + merge_recv[r, 2] * f_other
        value = (merge_send[c, r, 0] * f_own + merge_recv[r, 0] * f_other) / total
        value = value.astype(jnp.bfloat16)
        for h in range(q_heads):
            attention[r * tree:(r + 1) * tree, h * 128:(h + 1) * 128] = (
                value[h * tree:(h + 1) * tree])

    columns = w_out.shape[1] // OUT_CHUNKS

    def sib_copy(n):
        return remote(part.at[n, 1 - c], part_sib.at[n], sib_ssem.at[n], sib_rsem.at[n], sib)

    def y_copy(n):
        return remote(y_send.at[n], y_recv.at[n], y_ssem.at[n], y_rsem.at[n], ypart)

    def z_copy(n, k):
        return remote(z_send.at[n, hop(k)], z_recv.at[n, k - 1], z_ssem.at[n, k - 1],
                      z_rsem.at[n, k - 1], at(hop(k), y, c))

    def project(n):
        product = jnp.dot(attention[...], w_out[:, n * columns:(n + 1) * columns],
                          preferred_element_type=jnp.float32)
        for d in range(count):
            part[n, d % 2, d // 2 % 2, d // 4] = product[d * 8:(d + 1) * 8]
        sib_copy(n).start()

    def sum_pair(n):
        sib_copy(n).wait()
        away = part[n, c, 1 - y] + part_sib[n, 1 - y]
        y_send[n] = away.reshape(LINE * 8, columns).astype(jnp.bfloat16)
        y_copy(n).start()

    def sum_y(n):
        y_copy(n).wait()
        held = (part[n, c, y] + part_sib[n, y]) + y_recv[n].astype(jnp.float32).reshape(
            LINE, 8, columns)
        part_sib[n, 0] = held
        for d in range(LINE):
            z_send[n, d] = jnp.concatenate(
                [held[d, :, :columns // 2], held[d, :, columns // 2:]], axis=0).astype(jnp.bfloat16)
        for k in range(1, LINE):
            z_copy(n, k).start()

    for turn in range(OUT_CHUNKS + 2):
        if turn < OUT_CHUNKS:
            project(turn)
        if 1 <= turn <= OUT_CHUNKS:
            sum_pair(turn - 1)
        if turn >= 2:
            sum_y(turn - 2)
    for n in range(OUT_CHUNKS):
        total = part_sib[n, 0, z]
        for k in range(1, LINE):
            z_copy(n, k).wait()
            landed = z_recv[n, k - 1].astype(jnp.float32)
            total = total + jnp.concatenate([landed[:8], landed[8:]], axis=1)
        out[:, n * columns:(n + 1) * columns] = total.astype(jnp.bfloat16)

    for copy in sent:
        copy.wait_send()
    for distance in range(LINE):
        for side in (1, -1):
            @pl.when(on_line(z - side * distance) & on_line(z + side))
            def _():
                line_copy(distance, side).wait_send()

            if distance > 0:
                @pl.when(on_line(z - side * distance))
                def _():
                    fan_copy(distance, side, ypart, 1).wait_send()
                    fan_copy(distance, side, sib, 2).wait_send()


def fused_body(
    layer_input, input_norm_gain, query_weight, key_value_weight, output_weight,
    cached_key_value, adapter_down_weight, adapter_up_weight, request_adapter,
    adapter_storage_index, cached_length, parent_node,
):
    rows, model = layer_input.shape
    half = model // 2
    packed = layer_input.reshape(rows, 2, half).transpose(1, 0, 2).reshape(2 * rows, half)
    exponents = np.arange(64) * (2.0 / 128)
    inverse = jnp.asarray(np.exp(exponents * -math.log(rope_base))[None].astype(np.float32))
    bf, f32 = jnp.bfloat16, jnp.float32
    count = 16
    rank = adapter_up_weight.shape[1]
    ranks = adapter_down_weight.shape[1]
    cols = query_weight.shape[1] + key_value_weight.shape[1]
    columns = model // OUT_CHUNKS
    dma = pltpu.SemaphoreType.DMA
    n = OUT_CHUNKS
    scratch = [
        pltpu.VMEM(query_weight.shape, bf), pltpu.VMEM(key_value_weight.shape, bf),
        pltpu.VMEM(output_weight.shape, bf), pltpu.VMEM(cached_key_value.shape, bf),
        pltpu.VMEM((count, 2 * rows, half), bf), pltpu.VMEM((count * rows, model), bf),
        pltpu.VMEM(adapter_down_weight.shape, bf), pltpu.VMEM(adapter_up_weight.shape, bf),
        pltpu.VMEM((2, 2, 4, 2 * rank, cols), bf), pltpu.VMEM((2, 4, 2 * rank, cols), bf),
        pltpu.VMEM((2, 4, 2 * rank, cols), bf), pltpu.VMEM((4, 2 * rank, cols), bf),
        pltpu.VMEM((4, 2 * rank, cols), bf), pltpu.VMEM((3, 2 * rank, cols), bf),
        pltpu.VMEM((3, ranks, 128), bf), pltpu.VMEM((5, ranks, 128), bf),
        pltpu.VMEM((2, 2, 4, 64, 128), bf), pltpu.VMEM((2, 2, 32, 128), bf),
        pltpu.VMEM((2, 32, 128), bf), pltpu.VMEM((2, 32, 128), bf),
        pltpu.VMEM((2, 2, 3, 256, 128), f32), pltpu.VMEM((2, 3, 256, 128), f32),
        pltpu.VMEM((128, 512), bf),
        pltpu.VMEM((n, 2, 2, 4, 8, columns), f32), pltpu.VMEM((n, 2, 4, 8, columns), f32),
        pltpu.VMEM((n, 32, columns), bf), pltpu.VMEM((n, 32, columns), bf),
        pltpu.VMEM((n, 4, 16, columns // 2), bf), pltpu.VMEM((n, 3, 16, columns // 2), bf),
        dma((6,)), dma((6,)), dma((4, 2, 3)), dma((count,)), dma((5,)), dma((5,)), dma((5,)), dma((5,)),
        dma((2,)), dma((2,)), dma((2,)), dma((2,)), dma((2,)),
        dma((n,)), dma((n,)), dma((n,)), dma((n,)), dma((n, 3)), dma((n, 3)),
    ]
    smem = pl.BlockSpec(memory_space=pltpu.SMEM)
    vmem = pl.BlockSpec(memory_space=pltpu.VMEM)
    hbm = pl.BlockSpec(memory_space=pl.ANY)
    return pl.pallas_call(
        fused_kernel,
        out_shape=jax.ShapeDtypeStruct((rows, model), bf),
        in_specs=[smem] * 3 + [vmem] * 4 + [hbm] * 6,
        out_specs=vmem,
        scratch_shapes=scratch,
        compiler_params=pltpu.CompilerParams(
            collective_id=0, has_side_effects=True, vmem_limit_bytes=60 * 2**20),
        cost_estimate=pl.CostEstimate(
            flops=5 * 10**9, bytes_accessed=25 * 2**20, transcendentals=4 * 2**20),
        name="fused_layer",
    )(adapter_storage_index, request_adapter, cached_length, packed, input_norm_gain[None],
      parent_node, inverse, adapter_down_weight, adapter_up_weight,
      query_weight, key_value_weight, output_weight, cached_key_value)


def solution(mesh):
    in_specs = (
        P(("rep", "tp"), None),
        P(),
        P(None, "tp"),
        P(None, "tp"),
        P("tp", None),
        P(None, "rep", "tp", None),
        P("tp", None, None),
        P("tp", None, None),
        P("rep"),
        P(),
        P("rep"),
        P("rep", None),
    )
    out_specs = P(("rep", "tp"), None)
    fused = mesh.shape["tp"] == 16 and mesh.shape["rep"] == 2
    return jax.shard_map(fused_body if fused else body, mesh=mesh, in_specs=in_specs, out_specs=out_specs, check_vma=False)
```

```python
import math

import jax
import numpy as np
import jax.numpy as jnp
from jax import lax
from jax.experimental import pallas as pl
from jax.experimental.pallas import tpu as pltpu
from jax.sharding import PartitionSpec as P

KEY_HEADS = 8


epsilon = 1e-05
adapter_scale = 0.5
rope_base = 500000.0
masked_score = -1e30


def broadcast(block, axis, source):
    block = jnp.where(lax.axis_index(axis) == source, block, jnp.zeros_like(block))
    return lax.psum(block, axis)


def partner_2(value, axis, stride):
    mask = 2**stride
    pairs = [(source, source ^ mask) for source in range(lax.axis_size(axis))]
    return lax.ppermute(value, axis, pairs)


def for_sending(x):

    def short(part):
        return part.astype(jnp.bfloat16) if part.dtype == jnp.float32 else part

    return jax.tree.map(short, x)


def normalize(hidden_rows, input_norm_gain):
    widened = hidden_rows.astype(jnp.float32)
    squares_mean = jnp.mean(widened * widened, axis=-1, keepdims=True)
    return (widened * lax.rsqrt(squares_mean + epsilon) * input_norm_gain).astype(jnp.bfloat16)


def ancestors(parents):
    node_count = parents.shape[0]
    node_index = jnp.arange(node_count, dtype=jnp.int32)
    parent_hot = (parents[:, None] == node_index[None, :]).astype(jnp.float32)
    reached = jnp.maximum(parent_hot, jnp.eye(node_count, dtype=jnp.float32))
    for repeat in range(node_count.bit_length()):
        reached = jnp.minimum(jnp.dot(reached, reached, precision=lax.Precision.HIGHEST), 1.0)
    return reached


def rotate(vectors, positions):
    half_dim = vectors.shape[-1] // 2
    exponents = jnp.arange(half_dim, dtype=jnp.float32) * (2.0 / vectors.shape[-1])
    inverse = jnp.exp(exponents * -math.log(rope_base))
    angles = positions.astype(jnp.float32)[:, None, None] * inverse[None, None, :]
    cosine = jnp.cos(angles)
    sine_part = jnp.sin(angles)
    leading = vectors[..., :half_dim]
    second = vectors[..., half_dim:]
    return jnp.concatenate(
        [leading * cosine - second * sine_part, second * cosine + leading * sine_part], axis=-1
    )


def project_down(tree_token_rows, down_result):
    return lax.dot_general(
        tree_token_rows, down_result, (((1,), (1,)), ((), ())), preferred_element_type=jnp.float32
    ).astype(jnp.bfloat16)


def spread(per_head, offset, width, head_dim):
    expanded = jnp.repeat(per_head, head_dim, axis=1)
    return lax.dynamic_slice_in_dim(expanded, offset, width, 1)


def combine(own_state, other_state, offset, head_dim):
    width = own_state[0].shape[1]
    new_top = jnp.maximum(own_state[1], other_state[1])
    own_factor = jnp.exp(own_state[1] - new_top)
    other_factor = jnp.exp(other_state[1] - new_top)
    new_total = own_state[2] * own_factor + other_state[2] * other_factor
    new_values = own_state[0] * spread(own_factor, offset, width, head_dim) + other_state[
        0
    ] * spread(other_factor, offset, width, head_dim)
    return (new_values, new_top, new_total)


def partial_attention(queries, all_keys, all_values, usable, group_heads):
    scores = lax.dot_general(
        queries, all_keys, (((1,), (1,)), ((), ())), preferred_element_type=jnp.float32
    ) * all_keys.shape[1] ** (-0.5)
    mask_rows = jnp.repeat(usable, group_heads, axis=0)
    scores = jnp.where(mask_rows, scores, masked_score)
    row_top = jnp.max(scores, axis=1, keepdims=True)
    weights = jnp.where(mask_rows, jnp.exp(scores - row_top), 0.0)
    row_total = jnp.sum(weights, axis=1, keepdims=True)
    blended = jnp.dot(weights.astype(jnp.bfloat16), all_values, preferred_element_type=jnp.float32)
    return (blended, row_top, row_total)


def body(
    layer_input,
    input_norm_gain,
    query_weight,
    key_value_weight,
    output_weight,
    cached_key_value,
    adapter_down_weight,
    adapter_up_weight,
    request_adapter,
    adapter_storage_index,
    cached_length,
    parent_node,
):
    devices = lax.axis_size("tp")
    device = lax.axis_index("tp")
    model_dim = query_weight.shape[0]
    query_cols = query_weight.shape[1]
    pair_cols = key_value_weight.shape[1]
    storage_slot_list = adapter_down_weight.shape[0]
    total_rank = adapter_down_weight.shape[1]
    rank_size = total_rank // 3
    requests = request_adapter.shape[0]
    tree_size = parent_node.shape[1]
    head_dim = cached_key_value.shape[3]
    block_keys = cached_key_value.shape[2]
    kv_width = pair_cols * devices // 2
    group_size = devices // KEY_HEADS
    depth_levels = group_size.bit_length() - 1
    head_group = device // group_size
    member = device % group_size
    group_width = query_cols * group_size
    group_heads = group_width // head_dim
    tree_block = tree_size // group_size
    everyone = lax.all_gather(layer_input, "tp", axis=0, tiled=True)
    normed = normalize(everyone, input_norm_gain)
    kv_start = device * pair_cols
    is_value = kv_start >= kv_width
    query_blocks = []
    pair_blocks = []
    for request in range(requests):
        storage_slot_index = adapter_storage_index[request_adapter[request]]
        owner_index = storage_slot_index // storage_slot_list
        slot_local = storage_slot_index % storage_slot_list
        request_down = lax.dynamic_index_in_dim(adapter_down_weight, slot_local, 0, keepdims=False)
        request_up = lax.dynamic_index_in_dim(adapter_up_weight, slot_local, 0, keepdims=False)
        tree_token_rows = normed[request * tree_size : (request + 1) * tree_size]
        down_result, up_result = (
            broadcast(request_down, "tp", owner_index),
            broadcast(request_up, "tp", owner_index),
        )
        low_rank = project_down(tree_token_rows, down_result)
        query_update = jnp.dot(
            low_rank[:, :rank_size],
            lax.dynamic_slice_in_dim(up_result, device * query_cols, query_cols, 1),
            preferred_element_type=jnp.float32,
        )
        query_blocks.append(
            (
                jnp.dot(tree_token_rows, query_weight, preferred_element_type=jnp.float32)
                + adapter_scale * query_update
            ).astype(jnp.bfloat16)
        )
        pair_rank = jnp.where(
            is_value, low_rank[:, 2 * rank_size :], low_rank[:, rank_size : 2 * rank_size]
        )
        paired_update = jnp.dot(
            pair_rank,
            lax.dynamic_slice_in_dim(up_result, model_dim + kv_start, pair_cols, 1),
            preferred_element_type=jnp.float32,
        )
        pair_blocks.append(
            (
                jnp.dot(tree_token_rows, key_value_weight, preferred_element_type=jnp.float32)
                + adapter_scale * paired_update
            ).astype(jnp.bfloat16)
        )
    query_local = jnp.concatenate(query_blocks, axis=0)
    pair_local = jnp.concatenate(pair_blocks, axis=0)
    pair_all = lax.all_gather(pair_local, "tp", axis=1, tiled=True)
    query_group = query_local
    for section_bit in range(depth_levels):
        partner = partner_2(query_group, "tp", section_bit)
        upper_half = member // 2**section_bit % 2 == 1
        query_group = jnp.concatenate(
            [
                jnp.where(upper_half, partner, query_group),
                jnp.where(upper_half, query_group, partner),
            ],
            axis=1,
        )
    key_cols = lax.dynamic_slice_in_dim(pair_all, head_group * head_dim, head_dim, 1)
    value_cols = lax.dynamic_slice_in_dim(pair_all, kv_width + head_group * head_dim, head_dim, 1)
    block_index = member * block_keys + jnp.arange(block_keys, dtype=jnp.int32)
    value_parts = []
    top_parts = []
    total_parts = []
    for request in range(requests):
        reached = ancestors(parent_node[request])
        node_depth = jnp.sum(reached, axis=1).astype(jnp.int32) - 1
        positions = cached_length[request] + node_depth
        request_queries = query_group[request * tree_size : (request + 1) * tree_size]
        queries = (
            rotate(
                request_queries.astype(jnp.float32).reshape(tree_size, group_heads, head_dim),
                positions,
            )
            .astype(jnp.bfloat16)
            .reshape(tree_size * group_heads, head_dim)
        )
        request_keys = key_cols[request * tree_size : (request + 1) * tree_size]
        new_keys = (
            rotate(request_keys.astype(jnp.float32).reshape(tree_size, 1, head_dim), positions)
            .astype(jnp.bfloat16)
            .reshape(tree_size, head_dim)
        )
        tree_keys = lax.dynamic_slice_in_dim(new_keys, member * tree_block, tree_block, 0)
        tree_values = lax.dynamic_slice_in_dim(
            value_cols[request * tree_size : (request + 1) * tree_size],
            member * tree_block,
            tree_block,
            0,
        )
        tree_mask = lax.dynamic_slice_in_dim(reached, member * tree_block, tree_block, 1) > 0.5
        cache_mask = jnp.broadcast_to(
            (block_index < cached_length[request])[None, :], (tree_size, block_keys)
        )
        all_keys = jnp.concatenate([cached_key_value[0, request], tree_keys], axis=0)
        all_values = jnp.concatenate([cached_key_value[1, request], tree_values], axis=0)
        blended, row_top, row_total = partial_attention(
            queries,
            all_keys,
            all_values,
            jnp.concatenate([cache_mask, tree_mask], axis=1),
            group_heads,
        )
        value_parts.append(blended.reshape(tree_size, group_width))
        top_parts.append(row_top.reshape(tree_size, group_heads))
        total_parts.append(row_total.reshape(tree_size, group_heads))
    merged = (
        jnp.concatenate(value_parts, axis=0),
        jnp.concatenate(top_parts, axis=0),
        jnp.concatenate(total_parts, axis=0),
    )
    window = group_width // group_size
    zero_offset = jnp.zeros((), jnp.int32)
    for section_bit in range(depth_levels):
        other_state = partner_2(
            (for_sending(merged[0]), for_sending(merged[1]), for_sending(merged[2])),
            "tp",
            section_bit,
        )
        merged = combine(merged, other_state, zero_offset, head_dim)
    offset = member * window
    kept_values = lax.dynamic_slice_in_dim(merged[0], offset, window, 1)
    attention = (kept_values / spread(merged[2], offset, window, head_dim)).astype(jnp.bfloat16)
    summed = lax.psum_scatter(
        jnp.dot(attention, output_weight, preferred_element_type=jnp.float32),
        "tp",
        scatter_dimension=0,
        tiled=True,
    )
    return summed.astype(jnp.bfloat16)


MESH = pl.DeviceIdType.MESH
LINE, PAIR, CORES = 4, 2, 2
OUT_CHUNKS = 4
KEY_CHUNK = 2048
lowest = -1e29


def fused_kernel(
    slot_of, adapter_of, length_of, rows_in, gain, parents, inverse, down, up,
    query_weight, pair_weight, out_weight, cache, out,
    w_query, w_pair, w_out, kv_cache, rows_all, normed, down_here, up_here,
    up_send, up_sib, up_mid, up_y, up_low, up_z, low_send, low_recv,
    query_buf, pair_own, tree_keys, tree_values,
    merge_send, merge_recv, attention, part, part_sib, y_send, y_recv, z_send, z_recv,
    load_sem, rows_send, line_send, rows_recv, up_ssem, up_rsem, low_ssem, low_rsem,
    query_sem, pair_ssem, pair_rsem, merge_ssem, merge_rsem,
    sib_ssem, sib_rsem, y_ssem, y_rsem, z_ssem, z_rsem,
):
    me = lax.axis_index("tp")
    z, y, c = me // (PAIR * CORES), me // CORES % PAIR, me % CORES
    count = LINE * PAIR * CORES

    def at(zz, yy, cc):
        return (zz * PAIR + yy) * CORES + cc

    def hop(k):
        return (z + k) % LINE

    def remote(src, dst, ssem, rsem, target):
        return pltpu.make_async_remote_copy(
            src_ref=src, dst_ref=dst, send_sem=ssem, recv_sem=rsem,
            device_id={"tp": target}, device_id_type=MESH,
        )

    sib, ypart = at(z, y, 1 - c), at(z, 1 - y, c)
    loads = [
        pltpu.make_async_copy(a, b, load_sem.at[i])
        for i, (a, b) in enumerate([
            (up, up_here), (down, down_here), (query_weight, w_query),
            (pair_weight, w_pair), (cache, kv_cache), (out_weight, w_out)])
    ]
    for load in loads:
        load.start()
    barrier = pltpu.get_barrier_semaphore()
    for k in range(1, count):
        pl.semaphore_signal(
            barrier, inc=1, device_id={"tp": (me + k) % count}, device_id_type=MESH)
    rows_all[me] = rows_in[...]
    pl.semaphore_wait(barrier, count - 1)

    sent = []

    def push_rows(block, target):
        copy = remote(rows_all.at[block], rows_all.at[block],
                      rows_send.at[len(sent)], rows_recv.at[block], target)
        copy.start()
        sent.append(copy)

    def take_rows(block):
        remote(rows_all.at[block], rows_all.at[block], rows_send.at[0],
               rows_recv.at[block], sib).wait_recv()

    def line_copy(distance, side):
        block = at(z - side * distance, y, c)
        return remote(rows_all.at[block], rows_all.at[block],
                      line_send.at[distance, (side + 1) // 2, 0], rows_recv.at[block],
                      at(z + side, y, c))

    def fan_copy(distance, side, target, place):
        block = at(z - side * distance, y, c)
        return remote(rows_all.at[block], rows_all.at[block],
                      line_send.at[distance, (side + 1) // 2, place], rows_recv.at[block], target)

    def on_line(place):
        return (place >= 0) & (place < LINE)

    for side in (1, -1):
        @pl.when(on_line(z + side))
        def _():
            line_copy(0, side).start()
    push_rows(me, ypart)
    push_rows(me, sib)

    requests, tree = 2, 64
    rank, slots = up_here.shape[1], up_here.shape[0]
    q_cols, p_cols = w_query.shape[1], w_pair.shape[1]
    width = q_cols * count
    chosen = []
    for r in range(requests):
        slot = slot_of[adapter_of[r]]
        chosen.append([slot == me * slots + s for s in range(slots)])
    loads[0].wait()
    for r in range(requests):
        picked = jnp.zeros(up_here.shape[1:], up_here.dtype)
        for s in range(slots):
            picked = jnp.where(chosen[r][s], up_here[s], picked)
        for d in range(count):
            zz, yy, cc = d // 4, d // 2 % 2, d % 2
            up_send[cc, yy, zz, r * rank:(r + 1) * rank, :q_cols] = (
                picked[:, d * q_cols:(d + 1) * q_cols])
            up_send[cc, yy, zz, r * rank:(r + 1) * rank, q_cols:] = (
                picked[:, width + d * p_cols:width + (d + 1) * p_cols])
    up_first = remote(up_send.at[1 - c], up_sib, up_ssem.at[0], up_rsem.at[0], sib)
    up_first.start()

    for distance in range(1, LINE):
        for side in (1, -1):
            @pl.when(on_line(z - side * distance))
            def _():
                take_rows(at(z - side * distance, y, c))

                @pl.when(on_line(z + side))
                def _():
                    line_copy(distance, side).start()

                fan_copy(distance, side, ypart, 1).start()
                fan_copy(distance, side, sib, 2).start()

    up_first.wait()
    up_mid[...] = up_send[c] + up_sib[...]

    reached, cosines, sines = [], [], []
    node = lax.broadcasted_iota(jnp.int32, (tree, tree), 1)
    own = lax.broadcasted_iota(jnp.int32, (tree, tree), 0)
    unit = jnp.where(own == node, 1.0, 0.0).astype(jnp.bfloat16)
    for r in range(requests):
        hot = jnp.where((parents[r:r + 1] == own) | (own == node), 1.0, 0.0)
        hot = lax.dot_general(hot.astype(jnp.bfloat16), unit, (((0,), (0,)), ((), ())),
                              preferred_element_type=jnp.float32)
        for _ in range(tree.bit_length()):
            short = hot.astype(jnp.bfloat16)
            hot = jnp.minimum(
                jnp.dot(short, short, preferred_element_type=jnp.float32), 1.0)
        reached.append(hot)
        depth = jnp.sum(hot, axis=1, keepdims=True).astype(jnp.int32) - 1
        position = (depth + length_of[r]).astype(jnp.float32)
        angles = position * inverse[...]
        cosines.append(jnp.cos(angles))
        sines.append(jnp.sin(angles))

    half = rows_all.shape[2]

    def norm_chip(k):
        parts = []
        for j in range(2):
            block = rows_all[2 * k + j].astype(jnp.float32)
            squares = jnp.sum(block * block, axis=1, keepdims=True)
            scale = lax.rsqrt((squares[:8] + squares[8:]) / (2 * half) + epsilon)
            parts.append((block[:8] * scale, block[8:] * scale))
        for h in range(2):
            both = jnp.concatenate([parts[0][h], parts[1][h]], axis=0)
            cols = slice(h * half, (h + 1) * half)
            normed[pl.ds(pl.multiple_of(k * 16, 16), 16), cols] = (
                both * gain[:, cols]).astype(jnp.bfloat16)

    for k in range(LINE):
        block = at(hop(k), 1 - y, c)
        take_rows(block)
        push_rows(block, sib)
        take_rows(at(hop(k), y, 1 - c))
        norm_chip(hop(k) * PAIR + y)

    up_second = remote(up_mid.at[1 - y], up_y, up_ssem.at[1], up_rsem.at[1], ypart)
    up_second.start()

    for k in range(LINE):
        take_rows(at(hop(k), 1 - y, 1 - c))
        norm_chip(hop(k) * PAIR + 1 - y)

    nt = (((1,), (1,)), ((), ()))
    tn = (((0,), (0,)), ((), ()))
    loads[1].wait()
    token = lax.broadcasted_iota(jnp.int32, (1, requests * tree), 1)
    low = jnp.zeros((down_here.shape[1], requests * tree), jnp.float32)
    for s in range(slots):
        flag = jnp.where(token < tree, chosen[0][s].astype(jnp.int32),
                         chosen[1][s].astype(jnp.int32))
        value = lax.dot_general(down_here[s], normed[...], nt,
                                preferred_element_type=jnp.float32)
        low = jnp.where(flag == 1, value, low)
    low_send[0] = low.astype(jnp.bfloat16)
    first = remote(low_send.at[0], low_recv.at[0], low_ssem.at[0], low_rsem.at[0], sib)
    first.start()

    up_second.wait()
    up_low[...] = up_mid[y] + up_y[...]
    up_third = []
    for k in range(1, LINE):
        copy = remote(up_low.at[hop(k)], up_z.at[k - 1], up_ssem.at[1 + k], up_rsem.at[1 + k],
                      at(hop(k), y, c))
        copy.start()
        up_third.append(copy)

    loads[2].wait()
    loads[3].wait()
    steps = 4
    depth = w_query.shape[0] // steps
    q_acc = jnp.zeros((requests * tree, q_cols), jnp.float32)
    p_acc = jnp.zeros((requests * tree, p_cols), jnp.float32)
    pending = first
    thirds = []
    for step in range(steps):
        cut = slice(step * depth, (step + 1) * depth)
        q_acc += jnp.dot(normed[:, cut], w_query[cut], preferred_element_type=jnp.float32)
        p_acc += jnp.dot(normed[:, cut], w_pair[cut], preferred_element_type=jnp.float32)
        if step == 0:
            first.wait()
            low_send[1] = low_send[0] + low_recv[0]
            second = remote(low_send.at[1], low_recv.at[1], low_ssem.at[1], low_rsem.at[1], ypart)
            second.start()
        if step == 1:
            second.wait()
            low_send[2] = low_send[1] + low_recv[1]
            for k in range(1, LINE):
                copy = remote(low_send.at[2], low_recv.at[1 + k], low_ssem.at[1 + k],
                              low_rsem.at[1 + k], at(hop(k), y, c))
                copy.start()
                thirds.append(copy)
    for copy in thirds + up_third:
        copy.wait()
    low_all = low_send[2] + low_recv[2] + low_recv[3] + low_recv[4]
    up_all = up_low[z] + up_z[0] + up_z[1] + up_z[2]
    is_value = me >= count // 2
    q_heads = q_cols // 128

    def rotated(vectors, r):
        front, back = vectors[:, :tree], vectors[:, tree:]
        return jnp.concatenate(
            [front * cosines[r] - back * sines[r], back * cosines[r] + front * sines[r]], axis=1)

    for r in range(requests):
        rows = slice(r * tree, (r + 1) * tree)
        low_r = low_all[:, rows]
        up_r = up_all[r * rank:(r + 1) * rank]
        update = lax.dot_general(low_r[:rank], up_r[:, :q_cols], tn,
                                 preferred_element_type=jnp.float32)
        q_pre = (q_acc[rows] + adapter_scale * update).astype(jnp.bfloat16).astype(jnp.float32)
        for h in range(q_heads):
            query_buf[c, r, h] = rotated(q_pre[:, h * 128:(h + 1) * 128], r).astype(jnp.bfloat16)
        pair_low = jnp.where(is_value, low_r[2 * rank:], low_r[rank:2 * rank])
        update = lax.dot_general(pair_low, up_r[:, q_cols:], tn,
                                 preferred_element_type=jnp.float32)
        p_pre = (p_acc[rows] + adapter_scale * update).astype(jnp.bfloat16).astype(jnp.float32)
        final = jnp.where(is_value, p_pre, rotated(p_pre, r)).astype(jnp.bfloat16)
        for m in range(CORES):
            pair_own[m, r] = final[m * (tree // 2):(m + 1) * (tree // 2)]

    q_copy = remote(query_buf.at[c], query_buf.at[c], query_sem.at[0], query_sem.at[1], sib)
    q_copy.start()
    group = me % (count // 2)
    for is_v, landing in ((0, tree_keys), (1, tree_values)):
        for m in range(CORES):
            target = group * CORES + m

            @pl.when((is_value == (is_v == 1)) & (target != me))
            def _():
                remote(pair_own.at[m], landing, pair_ssem.at[m], pair_rsem.at[is_v], target).start()

            @pl.when((is_value == (is_v == 1)) & (target == me))
            def _():
                landing[...] = pair_own[m]

    for m in range(CORES):
        @pl.when(group * CORES + m != me)
        def _():
            remote(pair_own.at[m], tree_keys, pair_ssem.at[m], pair_rsem.at[0], sib).wait_send()

    @pl.when(me // CORES != me)
    def _():
        remote(pair_own.at[0], tree_keys, pair_ssem.at[0], pair_rsem.at[0], sib).wait_recv()

    @pl.when(me // CORES + count // 2 != me)
    def _():
        remote(pair_own.at[0], tree_values, pair_ssem.at[0], pair_rsem.at[1], sib).wait_recv()

    q_copy.wait_send()
    remote(query_buf.at[1 - c], query_buf.at[1 - c], query_sem.at[0], query_sem.at[1],
           sib).wait_recv()

    loads[4].wait()
    heads = CORES * q_heads
    block_rows = heads * tree
    scale = 128 ** -0.5
    slots_here = kv_cache.shape[2]
    for r in range(requests):
        queries = query_buf[:, r].reshape(block_rows, 128)
        mask = jnp.where(c == 0, reached[r][:, :tree // 2], reached[r][:, tree // 2:])
        mask = jnp.concatenate([mask] * heads, axis=0)
        scores = lax.dot_general(queries, tree_keys[r], nt,
                                 preferred_element_type=jnp.float32) * scale
        scores = jnp.where(mask > 0.5, scores, masked_score)
        top = jnp.maximum(jnp.max(scores, axis=1, keepdims=True), lowest)
        weights = jnp.exp(scores - top)
        total = jnp.sum(weights, axis=1, keepdims=True)
        blend = jnp.dot(weights.astype(jnp.bfloat16), tree_values[r],
                        preferred_element_type=jnp.float32)
        limit = length_of[r] - c * slots_here

        def key_step(j, carry):
            top, total, blend = carry
            start = pl.multiple_of(j * KEY_CHUNK, KEY_CHUNK)
            scores = lax.dot_general(queries, kv_cache[0, r, pl.ds(start, KEY_CHUNK)], nt,
                                     preferred_element_type=jnp.float32) * scale
            column = lax.broadcasted_iota(jnp.int32, (1, KEY_CHUNK), 1) + start
            scores = jnp.where(column < limit, scores, masked_score)
            new_top = jnp.maximum(top, jnp.max(scores, axis=1, keepdims=True))
            weights = jnp.exp(scores - new_top)
            factor = jnp.exp(top - new_top)
            total = total * factor + jnp.sum(weights, axis=1, keepdims=True)
            blend = blend * factor + jnp.dot(
                weights.astype(jnp.bfloat16), kv_cache[1, r, pl.ds(start, KEY_CHUNK)],
                preferred_element_type=jnp.float32)
            return new_top, total, blend

        top, total, blend = lax.fori_loop(0, slots_here // KEY_CHUNK, key_step,
                                          (top, total, blend))
        top = jnp.broadcast_to(top, blend.shape)
        total = jnp.broadcast_to(total, blend.shape)
        mine = block_rows // CORES
        for m in range(CORES):
            cut = slice(m * mine, (m + 1) * mine)
            merge_send[m, r, 0] = blend[cut]
            merge_send[m, r, 1] = top[cut]
            merge_send[m, r, 2] = total[cut]
        remote(merge_send.at[1 - c, r], merge_recv.at[r], merge_ssem.at[r], merge_rsem.at[r],
               sib).start()

    loads[5].wait()
    for r in range(requests):
        remote(merge_send.at[1 - c, r], merge_recv.at[r], merge_ssem.at[r], merge_rsem.at[r],
               sib).wait()
        top = jnp.maximum(merge_send[c, r, 1], merge_recv[r, 1])
        f_own, f_other = jnp.exp(merge_send[c, r, 1] - top), jnp.exp(merge_recv[r, 1] - top)
        total = merge_send[c, r, 2] * f_own + merge_recv[r, 2] * f_other
        value = (merge_send[c, r, 0] * f_own + merge_recv[r, 0] * f_other) / total
        value = value.astype(jnp.bfloat16)
        for h in range(q_heads):
            attention[r * tree:(r + 1) * tree, h * 128:(h + 1) * 128] = (
                value[h * tree:(h + 1) * tree])

    columns = w_out.shape[1] // OUT_CHUNKS

    def sib_copy(n):
        return remote(part.at[n, 1 - c], part_sib.at[n], sib_ssem.at[n], sib_rsem.at[n], sib)

    def y_copy(n):
        return remote(y_send.at[n], y_recv.at[n], y_ssem.at[n], y_rsem.at[n], ypart)

    def z_copy(n, k):
        return remote(z_send.at[n, hop(k)], z_recv.at[n, k - 1], z_ssem.at[n, k - 1],
                      z_rsem.at[n, k - 1], at(hop(k), y, c))

    def project(n):
        product = jnp.dot(attention[...], w_out[:, n * columns:(n + 1) * columns],
                          preferred_element_type=jnp.float32)
        for d in range(count):
            part[n, d % 2, d // 2 % 2, d // 4] = product[d * 8:(d + 1) * 8]
        sib_copy(n).start()

    def sum_pair(n):
        sib_copy(n).wait()
        away = part[n, c, 1 - y] + part_sib[n, 1 - y]
        y_send[n] = away.reshape(LINE * 8, columns).astype(jnp.bfloat16)
        y_copy(n).start()

    def sum_y(n):
        y_copy(n).wait()
        held = (part[n, c, y] + part_sib[n, y]) + y_recv[n].astype(jnp.float32).reshape(
            LINE, 8, columns)
        part_sib[n, 0] = held
        for d in range(LINE):
            z_send[n, d] = jnp.concatenate(
                [held[d, :, :columns // 2], held[d, :, columns // 2:]], axis=0).astype(jnp.bfloat16)
        for k in range(1, LINE):
            z_copy(n, k).start()

    for turn in range(OUT_CHUNKS + 2):
        if turn < OUT_CHUNKS:
            project(turn)
        if 1 <= turn <= OUT_CHUNKS:
            sum_pair(turn - 1)
        if turn >= 2:
            sum_y(turn - 2)
    for n in range(OUT_CHUNKS):
        total = part_sib[n, 0, z]
        for k in range(1, LINE):
            z_copy(n, k).wait()
            landed = z_recv[n, k - 1].astype(jnp.float32)
            total = total + jnp.concatenate([landed[:8], landed[8:]], axis=1)
        out[:, n * columns:(n + 1) * columns] = total.astype(jnp.bfloat16)

    for copy in sent:
        copy.wait_send()
    for distance in range(LINE):
        for side in (1, -1):
            @pl.when(on_line(z - side * distance) & on_line(z + side))
            def _():
                line_copy(distance, side).wait_send()

            if distance > 0:
                @pl.when(on_line(z - side * distance))
                def _():
                    fan_copy(distance, side, ypart, 1).wait_send()
                    fan_copy(distance, side, sib, 2).wait_send()


def fused_body(
    layer_input, input_norm_gain, query_weight, key_value_weight, output_weight,
    cached_key_value, adapter_down_weight, adapter_up_weight, request_adapter,
    adapter_storage_index, cached_length, parent_node,
):
    rows, model = layer_input.shape
    half = model // 2
    packed = layer_input.reshape(rows, 2, half).transpose(1, 0, 2).reshape(2 * rows, half)
    exponents = np.arange(64) * (2.0 / 128)
    inverse = jnp.asarray(np.exp(exponents * -math.log(rope_base))[None].astype(np.float32))
    bf, f32 = jnp.bfloat16, jnp.float32
    count = 16
    rank = adapter_up_weight.shape[1]
    ranks = adapter_down_weight.shape[1]
    cols = query_weight.shape[1] + key_value_weight.shape[1]
    columns = model // OUT_CHUNKS
    dma = pltpu.SemaphoreType.DMA
    n = OUT_CHUNKS
    scratch = [
        pltpu.VMEM(query_weight.shape, bf), pltpu.VMEM(key_value_weight.shape, bf),
        pltpu.VMEM(output_weight.shape, bf), pltpu.VMEM(cached_key_value.shape, bf),
        pltpu.VMEM((count, 2 * rows, half), bf), pltpu.VMEM((count * rows, model), bf),
        pltpu.VMEM(adapter_down_weight.shape, bf), pltpu.VMEM(adapter_up_weight.shape, bf),
        pltpu.VMEM((2, 2, 4, 2 * rank, cols), bf), pltpu.VMEM((2, 4, 2 * rank, cols), bf),
        pltpu.VMEM((2, 4, 2 * rank, cols), bf), pltpu.VMEM((4, 2 * rank, cols), bf),
        pltpu.VMEM((4, 2 * rank, cols), bf), pltpu.VMEM((3, 2 * rank, cols), bf),
        pltpu.VMEM((3, ranks, 128), bf), pltpu.VMEM((5, ranks, 128), bf),
        pltpu.VMEM((2, 2, 4, 64, 128), bf), pltpu.VMEM((2, 2, 32, 128), bf),
        pltpu.VMEM((2, 32, 128), bf), pltpu.VMEM((2, 32, 128), bf),
        pltpu.VMEM((2, 2, 3, 256, 128), f32), pltpu.VMEM((2, 3, 256, 128), f32),
        pltpu.VMEM((128, 512), bf),
        pltpu.VMEM((n, 2, 2, 4, 8, columns), f32), pltpu.VMEM((n, 2, 4, 8, columns), f32),
        pltpu.VMEM((n, 32, columns), bf), pltpu.VMEM((n, 32, columns), bf),
        pltpu.VMEM((n, 4, 16, columns // 2), bf), pltpu.VMEM((n, 3, 16, columns // 2), bf),
        dma((6,)), dma((6,)), dma((4, 2, 3)), dma((count,)), dma((5,)), dma((5,)), dma((5,)), dma((5,)),
        dma((2,)), dma((2,)), dma((2,)), dma((2,)), dma((2,)),
        dma((n,)), dma((n,)), dma((n,)), dma((n,)), dma((n, 3)), dma((n, 3)),
    ]
    smem = pl.BlockSpec(memory_space=pltpu.SMEM)
    vmem = pl.BlockSpec(memory_space=pltpu.VMEM)
    hbm = pl.BlockSpec(memory_space=pl.ANY)
    return pl.pallas_call(
        fused_kernel,
        out_shape=jax.ShapeDtypeStruct((rows, model), bf),
        in_specs=[smem] * 3 + [vmem] * 4 + [hbm] * 6,
        out_specs=vmem,
        scratch_shapes=scratch,
        compiler_params=pltpu.CompilerParams(
            collective_id=0, has_side_effects=True, vmem_limit_bytes=60 * 2**20),
        cost_estimate=pl.CostEstimate(
            flops=5 * 10**9, bytes_accessed=25 * 2**20, transcendentals=4 * 2**20),
        name="fused_layer",
    )(adapter_storage_index, request_adapter, cached_length, packed, input_norm_gain[None],
      parent_node, inverse, adapter_down_weight, adapter_up_weight,
      query_weight, key_value_weight, output_weight, cached_key_value)


def solution(mesh):
    in_specs = (
        P(("rep", "tp"), None),
        P(),
        P(None, "tp"),
        P(None, "tp"),
        P("tp", None),
        P(None, "rep", "tp", None),
        P("tp", None, None),
        P("tp", None, None),
        P("rep"),
        P(),
        P("rep"),
        P("rep", None),
    )
    out_specs = P(("rep", "tp"), None)
    fused = mesh.shape["tp"] == 16 and mesh.shape["rep"] == 2
    return jax.shard_map(fused_body if fused else body, mesh=mesh, in_specs=in_specs, out_specs=out_specs, check_vma=False)
```
